512 devices in a mesh: vol: 32 (over x, z), nar: 16 (over y, core).
Axes of the slice: x: 4, y: 8, z: 8, core: 2. Of those that a mesh axis runs over, the one named last changes fastest.
Arguments:
- series: bfloat16 [32768, 2048], P(('vol', 'nar')), may hold values from -6 to 6
- send_rows: int32 [32, 16, 64], P('vol', 'nar'), may hold values from -1 to 63, as said below
- bin_counts: int32 [16], replicated, may hold values from 1 to 32, 256 in all
- observer_cells: int32 [2, 512], replicated, may hold values from 0 to 127
Outputs:
- spectra_out: float32 [16, 32, 2, 512], P('nar', 'vol')
The draws below stay inside these ranges and needn't reach their ends.
Inputs may be any that keep to these rules, and one draw needn't show every extreme that they name: `send_rows`: entry (u, n, k) names the row of device (u, n)'s 64 rows of series for slot k mod 2 bound for the patch owner at vol index k // 2 and nar index n, or is -1 for an empty slot; one device never names a row twice. Nar index m owns bin_counts[m] bins in order, from the sum of the counts before m on; some owner holds exactly 32 bins. `observer_cells`: row 0 holds polar indices, row 1 azimuthal indices.
All inputs are finite; a program needn't handle non-finite values.
Results may differ from the reference program's by a relative error of at most 0.0043.
Values may be sent and summed in bfloat16 or wider, within the bound.
A program may use at most 64 MiB of HBM per device.

```python
import math
import jax
import jax.numpy as jnp
import numpy as np
from jax import lax

NT = 512
NF = 256
NQ = 4
CAP = 2
VROWS = 64
OBS = 512
FCAP = 32
N_VOL = 32
N_NAR = 16


def draw_send_rows(key, part):
    slot_total = N_VOL * CAP
    key_list = jax.random.split(jax.random.fold_in(key, 11), N_VOL * N_NAR)
    chosen = jax.vmap(lambda single: jax.random.permutation(single, VROWS)[:slot_total])(key_list)
    occupied = jax.random.randint(jax.random.fold_in(key, 12), (N_VOL * N_NAR, slot_total), 0, 5) < 3
    return jnp.where(occupied, chosen, -1).astype(jnp.int32).reshape(N_VOL, N_NAR, slot_total)


def plant(drawn, key, smallest, top_value):
    longest = drawn.shape.index(max(drawn.shape))
    spots = []
    for shift in (0, 1):
        where = [jax.random.randint(jax.random.fold_in(key, axis), (), 0, length) for axis, length in enumerate(drawn.shape)]
        where[longest] = (where[longest] + shift) % drawn.shape[longest]
        spots.append(tuple(where))
    return drawn.at[spots[0]].set(smallest).at[spots[1]].set(top_value)


def level_of(key, dims, shards, smallest, high):
    level, own = 1.0, jax.random.fold_in(key, 6)
    for axis_at, blocks in shards:
        draws = jnp.exp(jax.random.uniform(jax.random.fold_in(own, axis_at), (blocks,), jnp.float32, smallest / len(shards), high / len(shards)))
        level = level * jnp.repeat(draws, dims[axis_at] // blocks).reshape([-1 if axis == axis_at else 1 for axis in range(len(dims))])
    return level


def length_profile(amount, total, reach, slope):
    weights = [(1 << 20) // math.isqrt(standing ** slope) + 1 for standing in range(2, amount + 1)]
    surplus, counts = total - reach - (amount - 1), [1] * (amount - 1)
    while surplus > 0:
        movable = [i for i in range(amount - 1) if counts[i] < reach]
        mass, budget = sum([weights[i] for i in movable]), surplus
        for i in movable:
            more = min(reach - counts[i], max(1, budget * weights[i] // mass), surplus)
            counts[i] = counts[i] + more
            surplus = surplus - more
    return np.array([reach] + counts)


def uneven(stream_key, count, total, bound, slope):
    if count == 2:
        one = jax.random.randint(stream_key, (), max(1, total - bound), min(bound, total - 1) + 1)
        return jnp.stack([one, total - one])
    tallies = jnp.asarray(length_profile(count, total, bound, slope), jnp.int32)
    twos = (count - 1) // 2
    donor, sink = tallies[1:1 + 2 * twos:2], tallies[2:2 + 2 * twos:2]
    room = jnp.minimum(donor - 1, bound - sink)
    moved = jax.random.randint(jax.random.fold_in(stream_key, 1), (twos,), 0, 1 << 20) % (room + 1)
    tallies = tallies.at[1:1 + 2 * twos:2].set(donor - moved).at[2:2 + 2 * twos:2].set(sink + moved)
    return tallies[jax.random.permutation(jax.random.fold_in(stream_key, 2), count)]


def normal_values(rng, extent, scale, limit, cuts=(), held_as=jnp.bfloat16):
    loudness = level_of(rng, extent, cuts, -0.22, 0.18) if cuts else 1.0
    entries = jax.random.normal(rng, extent, jnp.float32) * scale * loudness
    return jnp.minimum(jnp.maximum(entries, -limit), limit).astype(held_as)


def setup_inputs(seed: int = 0) -> dict:
    arg_keys = jax.random.split(jax.random.key(seed), 5)
    series = normal_values(arg_keys[0], (N_VOL * N_NAR * VROWS, NQ * NT), 1.0, 6.0, ((0, 512),))
    send_rows = draw_send_rows(jax.random.fold_in(arg_keys[4], 71), 0)
    bin_counts = uneven(arg_keys[2], N_NAR, NF, FCAP, 2).astype(jnp.int32)
    observer_cells = plant(jax.random.randint(arg_keys[3], (2, OBS), 0, 128), jax.random.fold_in(arg_keys[3], 1), 0, 127).astype(jnp.int32)
    return dict(series=series, send_rows=send_rows, bin_counts=bin_counts, observer_cells=observer_cells)


WAVE_STEP = 0.05

def dft_table(bin_ids, keep_bin, time_len):
    time_steps = jnp.arange(time_len, dtype=jnp.int32)
    frequency = bin_ids.astype(jnp.int32) + 1
    phase_turns = time_steps[:, None] * frequency[None, :] % time_len
    angle_grid = phase_turns.astype(jnp.float32) * (2.0 * math.pi / time_len)
    dft_grid = jnp.stack([jnp.cos(angle_grid), -jnp.sin(angle_grid)], axis=-1)
    dft_grid = jnp.where(keep_bin[None, :, None], dft_grid, jnp.float32(0.0))
    return dft_grid.reshape(time_len, 2 * bin_ids.shape[0]).astype(jnp.bfloat16)

def positions(point_list):
    point_list = point_list.astype(jnp.int32)
    beside_all = (point_list * 1597 % 8191).astype(jnp.float32) * (2.0 * math.pi / 8191.0)
    jitter = (point_list * 613 % 127).astype(jnp.float32) * (0.37 / 127.0)
    axial = (point_list // 128).astype(jnp.float32) * 0.5 + jitter
    return (20.0 * jnp.cos(beside_all), 20.0 * jnp.sin(beside_all), axial)

def directions(obs_cells):
    polar_angle = (obs_cells[0].astype(jnp.float32) + 0.5) * (math.pi / 128.0)
    azimuth = obs_cells[1].astype(jnp.float32) * (2.0 * math.pi / 128.0)
    return (jnp.sin(polar_angle) * jnp.cos(azimuth), jnp.sin(polar_angle) * jnp.sin(azimuth), jnp.cos(polar_angle))

def project(facing, place_xyz):
    dotted = facing[0][:, None] * place_xyz[0][None, :] + facing[1][:, None] * place_xyz[1][None, :]
    return dotted + facing[2][:, None] * place_xyz[2][None, :]

def kernels(bin_ids, dotted):
    wavenumber = (bin_ids.astype(jnp.float32) + 1.0) * WAVE_STEP
    phase_grid = wavenumber[:, None, None] * dotted[None]
    return jnp.concatenate([jnp.cos(phase_grid), jnp.sin(phase_grid)], axis=1).astype(jnp.bfloat16)

def combine(products, bin_ids, facing, norm_scale):
    observers = facing[0].shape[0]
    bin_total = bin_ids.shape[0]
    cos_part = products[:, :observers].reshape(bin_total, observers, NQ, 2)
    sine_part = products[:, observers:].reshape(bin_total, observers, NQ, 2)
    real_part = cos_part[..., 0] + sine_part[..., 1]
    imag_part = cos_part[..., 1] - sine_part[..., 0]
    weights = jnp.stack([jnp.ones_like(facing[0]), facing[0], facing[1], facing[2]], axis=-1)
    real_sum = lax.optimization_barrier(jnp.sum(real_part * weights[None], axis=-1))
    imag_sum = lax.optimization_barrier(jnp.sum(imag_part * weights[None], axis=-1))
    amplitude = (bin_ids.astype(jnp.float32) + 1.0) * (norm_scale / NF)
    return jnp.stack([-amplitude[:, None] * imag_sum, amplitude[:, None] * real_sum], axis=1)

def reference(series, send_rows, bin_counts, observer_cells):
    slot_total = send_rows.shape[2]
    listing = send_rows.reshape(-1)
    point_total = listing.shape[0]
    point_ids = jnp.arange(point_total, dtype=jnp.int32)
    source_rows = point_ids // slot_total * VROWS + jnp.maximum(listing, 0)
    surface_rows = jnp.where((listing >= 0)[:, None], series[source_rows], jnp.zeros((), series.dtype))
    time_len = series.shape[1] // NQ
    all_bins = jnp.arange(NF, dtype=jnp.int32)
    dft_grid = dft_table(all_bins, all_bins >= 0, time_len)
    spectra = jnp.dot(surface_rows.reshape(point_total * NQ, time_len), dft_grid, preferred_element_type=jnp.float32)
    spectra = (spectra * (1.0 / math.sqrt(time_len))).astype(jnp.bfloat16)
    spectra = spectra.reshape(point_total, NQ, NF, 2).transpose(2, 1, 3, 0).reshape(NF, 2 * NQ, point_total)
    facing = directions(observer_cells)
    dotted = project(facing, positions(point_ids))
    norm_scale = 1.0 / math.sqrt(point_total)

    def one_bin(bin_id):
        one_id = bin_id[None]
        green_grid = kernels(one_id, dotted).astype(jnp.float32)
        spec_one = lax.dynamic_index_in_dim(spectra, bin_id, 0, keepdims=True).astype(jnp.float32)
        products = jnp.einsum('bxp,bcp->bxc', green_grid, spec_one, precision=lax.Precision.HIGHEST)
        return combine(products, one_id, facing, norm_scale)[0]
    full_spectra = lax.map(one_bin, all_bins)
    starts = jnp.cumsum(bin_counts) - bin_counts
    slot_ids = jnp.arange(N_NAR * FCAP, dtype=jnp.int32)
    owner_slot = slot_ids // FCAP
    within = slot_ids % FCAP
    chosen_bin = jnp.minimum(starts[owner_slot] + within, NF - 1)
    valid_slot = within < bin_counts[owner_slot]
    result = jnp.where(valid_slot[:, None, None], full_spectra[chosen_bin], jnp.float32(0.0))
    return result.reshape(N_NAR, FCAP, 2, full_spectra.shape[-1])
```

```python
import math

import jax
import jax.numpy as jnp
from jax import lax
from jax.sharding import PartitionSpec as P

NF = 256
NQ = 4


WAVE_STEP = 0.05


def dft_table(bin_ids, keep_bin, time_len):
    time_steps = jnp.arange(time_len, dtype=jnp.int32)
    frequency = bin_ids + 1
    phase_turns = time_steps[:, None] * frequency[None, :] % time_len
    angle_grid = phase_turns.astype(jnp.float32) * (2.0 * math.pi / time_len)
    dft_grid = jnp.stack([jnp.cos(angle_grid), -jnp.sin(angle_grid)], axis=-1)
    dft_grid = jnp.where(keep_bin[None, :, None], dft_grid, jnp.float32(0.0))
    return dft_grid.reshape(time_len, 2 * bin_ids.shape[0]).astype(jnp.bfloat16)


def positions(point_list):
    beside_all = (point_list * 1597 % 8191).astype(jnp.float32) * (2.0 * math.pi / 8191.0)
    jitter = (point_list * 613 % 127).astype(jnp.float32) * (0.37 / 127.0)
    axial = (point_list // 128).astype(jnp.float32) * 0.5 + jitter
    return (20.0 * jnp.cos(beside_all), 20.0 * jnp.sin(beside_all), axial)


def directions(obs_cells):
    polar_angle = (obs_cells[0].astype(jnp.float32) + 0.5) * (math.pi / 128.0)
    azimuth = obs_cells[1].astype(jnp.float32) * (2.0 * math.pi / 128.0)
    return (
        jnp.sin(polar_angle) * jnp.cos(azimuth),
        jnp.sin(polar_angle) * jnp.sin(azimuth),
        jnp.cos(polar_angle),
    )


def project(facing, place_xyz):
    dotted = facing[0][:, None] * place_xyz[0][None, :] + facing[1][:, None] * place_xyz[1][None, :]
    return dotted + facing[2][:, None] * place_xyz[2][None, :]


def kernels(bin_ids, dotted):
    wavenumber = (bin_ids.astype(jnp.float32) + 1.0) * WAVE_STEP
    phase_grid = wavenumber[:, None, None] * dotted[None]
    return jnp.concatenate([jnp.cos(phase_grid), jnp.sin(phase_grid)], axis=1).astype(jnp.bfloat16)


def combine(products, bin_ids, facing, norm_scale):
    observers = facing[0].shape[0]
    bin_total = bin_ids.shape[0]
    cos_part = products[:, :observers].reshape(bin_total, observers, NQ, 2)
    sine_part = products[:, observers:].reshape(bin_total, observers, NQ, 2)
    real_part = cos_part[..., 0] + sine_part[..., 1]
    imag_part = cos_part[..., 1] - sine_part[..., 0]
    weights = jnp.stack([jnp.ones_like(facing[0]), facing[0], facing[1], facing[2]], axis=-1)
    real_sum = jnp.sum(real_part * weights[None], axis=-1)
    imag_sum = jnp.sum(imag_part * weights[None], axis=-1)
    amplitude = (bin_ids.astype(jnp.float32) + 1.0) * (norm_scale / NF)
    return jnp.stack([-amplitude[:, None] * imag_sum, amplitude[:, None] * real_sum], axis=1)


def apply_green(bin_ids, spec_block, dotted, facing, norm_scale):
    green_grid = kernels(bin_ids, dotted)
    products = jnp.einsum(
        "bxp,bcp->bxc", green_grid, spec_block, preferred_element_type=jnp.float32
    )
    return combine(products, bin_ids, facing, norm_scale)


def per_device(series, send_rows, bin_counts, observer_cells):
    vol_count = lax.axis_size("vol")
    nar_count = lax.axis_size("nar")
    vol_index = lax.axis_index("vol")
    nar_index = lax.axis_index("nar")
    bin_cap = vol_count * max(1, 2 * NF // (nar_count * vol_count))
    time_len = series.shape[1] // NQ
    slot_total = send_rows.shape[2]
    slot_width = slot_total // vol_count
    listing = send_rows.reshape(-1)
    picked = jnp.take(series, jnp.maximum(listing, 0), axis=0)
    packed = jnp.where((listing >= 0)[:, None], picked, jnp.zeros((), series.dtype))
    arrived = lax.all_to_all(packed, "vol", split_axis=0, concat_axis=0, tiled=True)
    owners = jnp.arange(bin_counts.shape[0], dtype=jnp.int32)
    starts = jnp.sum(jnp.where(owners[None, :] < owners[:, None], bin_counts[None, :], 0), axis=1)
    own_start = starts[nar_index]
    own_count = bin_counts[nar_index]
    dft_scale = 1.0 / math.sqrt(time_len)
    within = jnp.arange(bin_cap, dtype=jnp.int32)
    own_table = dft_table(own_start + within, within < own_count, time_len)
    row_piece = lax.all_gather(arrived, "nar", axis=0, tiled=True)
    rows_here = row_piece.shape[0]
    spectral = jnp.dot(
        row_piece.reshape(rows_here * NQ, time_len), own_table, preferred_element_type=jnp.float32
    )
    spectral = (spectral * dft_scale).astype(jnp.bfloat16).reshape(rows_here, NQ, bin_cap, 2)
    spectra = spectral.transpose(2, 1, 3, 0).reshape(bin_cap, 2 * NQ, rows_here)
    local_points = nar_count * slot_total
    norm_scale = 1.0 / math.sqrt(vol_count * nar_count * slot_total)
    facing = directions(observer_cells)
    share_rows = bin_cap // vol_count
    local_index = jnp.arange(local_points, dtype=jnp.int32)
    nar_source = local_index // slot_total
    remain = local_index % slot_total
    vol_source = remain // slot_width
    within_slot = remain % slot_width
    dotted = project(
        facing,
        positions(
            ((vol_source * nar_count + nar_source) * vol_count + vol_index) * slot_width
            + within_slot
        ),
    )
    row_count = lax.axis_size("vol") * share_rows
    bin_ids = own_start + jnp.arange(row_count, dtype=jnp.int32)
    group_size = 4

    def one_group(bundle):
        return apply_green(bundle[0], bundle[1], dotted, facing, norm_scale)

    grouped = lax.map(
        one_group,
        (
            bin_ids.reshape(row_count // group_size, group_size),
            spectra.reshape(row_count // group_size, group_size, 2 * NQ, local_points),
        ),
    )
    result = lax.psum_scatter(
        grouped.reshape(row_count, 2, grouped.shape[-1]), "vol", scatter_dimension=0, tiled=True
    )
    return result.reshape(1, share_rows, 2, result.shape[-1])


def solution(mesh):
    placed = (P(("vol", "nar"), None), P("vol", "nar", None), P(), P())
    return jax.shard_map(
        per_device,
        mesh=mesh,
        in_specs=placed,
        out_specs=P("nar", "vol", None, None),
        check_vma=False,
    )
```

```python
import math

import jax
import jax.numpy as jnp
import ml_dtypes
import numpy as np
from jax import lax
from jax.experimental import pallas as pl
from jax.experimental.pallas import tpu as pltpu
from jax.sharding import PartitionSpec as P

NT = 512
NF = 256
NQ = 4
OBS = 512
WAVE_STEP = 0.05
BF = jnp.bfloat16
F32 = jnp.float32
MESH = pl.DeviceIdType.MESH


def dft_rows():
    steps = np.arange(NT, dtype=np.int64)
    turns = (np.arange(1, NF + 1, dtype=np.int64)[:, None] * steps[None, :]) % NT
    angle = turns.astype(np.float32) * np.float32(2.0 * math.pi / NT)
    table = np.stack([np.cos(angle), -np.sin(angle)], axis=1)
    return table.reshape(2 * NF, NT).astype(ml_dtypes.bfloat16)


SIN_TERMS = [(-1.0) ** i / math.factorial(2 * i + 1) for i in range(7)]
COS_TERMS = [(-1.0) ** i / math.factorial(2 * i) for i in range(8)]


def polynomial(terms, square):
    total = terms[-1]
    for term in terms[-2::-1]:
        total = total * square + term
    return total


def cos_sin(turns):
    half = (turns - jnp.round(turns)) * math.pi
    square = half * half
    s = half * polynomial(SIN_TERMS, square)
    c = polynomial(COS_TERMS, square)
    return 1.0 - 2.0 * s * s, 2.0 * s * c


def times(one, other):
    return one[0] * other[0] - one[1] * other[1], one[0] * other[1] + one[1] * other[0]


def squared(one):
    return 1.0 - 2.0 * one[1] * one[1], 2.0 * one[0] * one[1]


def modulo(value, base):
    rest = value - (value.astype(F32) * (1.0 / base)).astype(jnp.int32) * base
    rest = jnp.where(rest < 0, rest + base, rest)
    return jnp.where(rest >= base, rest - base, rest)


def kernel(
    counts_ref,
    series_ref,
    listing_ref,
    cells_ref,
    dft_ref,
    out_ref,
    spec,
    own,
    swap_out,
    swap_in,
    place,
    facing,
    weight,
    table,
    coef,
    stage,
    part_out,
    part_in,
    slot_out,
    slot_in,
    last_out,
    last_in,
    swap_sems,
    part_sems,
    slot_sems,
    last_sems,
):
    u = lax.axis_index("vol")
    n = lax.axis_index("nar")
    x, z = u // 8, u % 8
    core = n % 2
    vols, nars = 32, 16

    barrier = pltpu.get_barrier_semaphore()

    def greet_vol(k, carry):
        pl.semaphore_signal(barrier, inc=1, device_id={"vol": (u + k) % vols}, device_id_type=MESH)
        return carry

    def greet_nar(k, carry):
        pl.semaphore_signal(barrier, inc=1, device_id={"nar": (n + k) % nars}, device_id_type=MESH)
        return carry

    lax.fori_loop(1, vols, greet_vol, 0)
    lax.fori_loop(1, nars, greet_nar, 0)

    rows = jnp.concatenate([series_ref[:, q * NT : (q + 1) * NT] for q in range(NQ)], axis=0)
    spectra = lax.dot_general(
        dft_ref[...], rows, (((1,), (1,)), ((), ())), preferred_element_type=F32
    )
    spectra = (spectra * (1.0 / math.sqrt(NT))).astype(BF)
    listing = listing_ref[...]
    listing = jnp.concatenate([listing, listing], axis=1)
    slot = lax.broadcasted_iota(jnp.int32, (256, 128), 1)
    line = lax.broadcasted_iota(jnp.int32, (256, 128), 0)
    mine = (slot // 64 == core) & (line % 64 == listing)
    for q in range(NQ):
        pick = jnp.where(mine & (line // 64 == q), 1.0, 0.0).astype(BF)
        spec[pl.ds(q, 2 * NF, stride=NQ), :] = jnp.dot(spectra, pick, preferred_element_type=F32)
    swap_out[...] = spec[pl.ds(pl.multiple_of((1 - core) * 1024, 1024), 1024), :].astype(BF)

    pl.semaphore_wait(barrier, vols + nars - 2)
    swap = pltpu.make_async_remote_copy(
        src_ref=swap_out,
        dst_ref=swap_in,
        send_sem=swap_sems.at[0],
        recv_sem=swap_sems.at[1],
        device_id={"nar": n + 1 - 2 * core},
        device_id_type=MESH,
    )
    swap.start()

    slab = u * 8 + n // 2
    point = slab * 128 + lax.broadcasted_iota(jnp.int32, (128, 128), 0)
    c, s = cos_sin(modulo(point * 1597, 8191).astype(F32) * (1.0 / 8191.0))
    place[0] = 20.0 * c
    place[1] = 20.0 * s
    place[2] = slab.astype(F32) * 0.5 + modulo(point * 613, 127).astype(F32) * (0.37 / 127.0)
    cells = cells_ref[...].astype(F32)
    polar = cos_sin((cells[0:1] + 0.5) * (1.0 / 256.0))
    azimuth = cos_sin(cells[1:2] * (1.0 / 128.0))
    facing[0] = jnp.broadcast_to(polar[1] * azimuth[0], (8, OBS))
    facing[1] = jnp.broadcast_to(polar[1] * azimuth[1], (8, OBS))
    facing[2] = jnp.broadcast_to(polar[0], (8, OBS))
    term = lax.broadcasted_iota(jnp.int32, (8, OBS), 0) % NQ
    weight[...] = jnp.where(
        term == 0,
        1.0,
        jnp.where(term == 1, facing[0], jnp.where(term == 2, facing[1], facing[2])),
    )

    def fill(at, carry):
        rows16 = pl.ds(pl.multiple_of((at // 2) * 16, 16), 16)
        lanes = pl.ds(pl.multiple_of((at % 2) * 256, 256), 256)
        dotted = 0.0
        for axis in range(3):
            spot = place[axis, rows16, :]
            look = facing[axis, :, lanes]
            dotted = dotted + jnp.concatenate([spot, spot], axis=1) * jnp.concatenate([look, look], axis=0)
        turns = dotted * (WAVE_STEP / (2.0 * math.pi))

        def keep(index, value):
            table[index, rows16, lanes] = value[0].astype(BF)
            table[index + 1, rows16, lanes] = value[1].astype(BF)

        fine = cos_sin(turns * 0.5)
        step = squared(fine)
        keep(16, fine)
        for i in range(1, 8):
            fine = times(fine, step)
            keep(16 + 2 * i, fine)
        for _ in range(4):
            step = squared(step)
        coarse = cos_sin(turns * (core.astype(F32) * 128.0 + 8.5))
        keep(0, coarse)
        for g in range(1, 8):
            coarse = times(coarse, step)
            keep(2 * g, coarse)
        return carry

    lax.fori_loop(0, 16, fill, 0)

    swap.wait()
    base = core * 1024

    def join(at, carry):
        here = pl.multiple_of(at * 64, 64)
        own[pl.ds(here, 64), :] = (
            spec[pl.ds(pl.multiple_of(base + here, 64), 64), :] + swap_in[pl.ds(here, 64), :].astype(F32)
        )
        return carry

    lax.fori_loop(0, 16, join, 0)
    sign = jnp.where(lax.broadcasted_iota(jnp.int32, (8, 128), 0) < 4, 1.0, -1.0)

    def lay(g, carry):
        for i in range(8):
            high = own[pl.ds(pl.multiple_of((16 * g + 8 + i) * 8, 8), 8), :]
            low = own[pl.ds(pl.multiple_of((16 * g + 7 - i) * 8, 8), 8), :]
            high2 = pltpu.roll(high, 4, 0) * sign
            low2 = pltpu.roll(low, 4, 0) * sign
            blocks = ((high, low), (-high, low), (high2, low2), (high2, -low2))
            for k, both in enumerate(blocks):
                coef[i, g, :, pl.ds(k * 128, 128)] = jnp.concatenate(both, axis=0).astype(BF)
        return carry

    lax.fori_loop(0, 8, lay, 0)

    def one_fine(step, carry):
        i = (step + z) % 8
        for g in range(8):
            for half in range(2):
                lanes = pl.ds(half * 256, 256)
                c, s = table[2 * g, :, lanes], table[2 * g + 1, :, lanes]
                fc, fs = table[16 + 2 * i, :, lanes], table[17 + 2 * i, :, lanes]
                green = jnp.concatenate([c * fc, s * fs, s * fc, c * fs], axis=0)
                sums = jnp.dot(coef[i, g], green, preferred_element_type=F32)
                for sg in range(2):
                    total = sums[8 * sg : 8 * sg + 8] * weight[:, lanes]
                    total = total + pltpu.roll(total, 7, 0)
                    total = total + pltpu.roll(total, 6, 0)
                    stage[sg, 2 * g : 2 * g + 1, lanes] = total[4:5]
                    stage[sg, 2 * g + 1 : 2 * g + 2, lanes] = total[0:1]
        for sg in range(2):
            for k in range(4):
                part_out[(step * 2 + sg) * 4 + k] = stage[sg, :, k * 128 : (k + 1) * 128].astype(BF)
        for sg in range(2):
            zt = i if sg == 0 else 7 - i
            for k in range(4):
                xt = (x + k) % 4
                source = part_out.at[(step * 2 + sg) * 4 + xt]
                target = part_in.at[sg, u]

                def send(source=source, target=target, ut=xt * 8 + zt):
                    pltpu.make_async_remote_copy(
                        src_ref=source,
                        dst_ref=target,
                        send_sem=part_sems.at[0],
                        recv_sem=part_sems.at[1],
                        device_id={"vol": ut},
                        device_id_type=MESH,
                    ).start()

                if k:
                    send()
                else:
                    pl.when(zt != z)(send)

                    @pl.when(zt == z)
                    def _(source=source, target=target):
                        pltpu.make_async_copy(source, target, part_sems.at[1]).start()

        return carry

    lax.fori_loop(0, 8, one_fine, 0)

    row = lax.broadcasted_iota(jnp.int32, (128, 32), 0)
    col = lax.broadcasted_iota(jnp.int32, (128, 32), 1)
    bin_of = core * 128 + ((col % 16) // 2 * 2 + 1 - col // 16) * 8 + z
    begin, begins, counts = jnp.int32(0), jnp.zeros_like(row), jnp.zeros_like(row)
    own_begin = jnp.int32(0)
    for m in range(nars):
        amount = counts_ref[m]
        begins = jnp.where(row // 8 == m, begin, begins)
        counts = jnp.where(row // 8 == m, amount, counts)
        own_begin = own_begin + jnp.where(m < n, amount, 0)
        begin = begin + amount
    seat = bin_of - begins
    ahead = seat - (row % 8) // 2 * 8
    chosen = (row % 2 == col % 2) & (ahead >= 0) & (ahead < 8) & (seat < counts)
    chosen = jnp.where(chosen, 1.0, 0.0).astype(BF)

    pltpu.make_async_copy(part_in, part_in, part_sems.at[1]).wait()
    sums = []
    for sg in range(2):

        def add(at, total, sg=sg):
            return total + part_in[sg, at].astype(F32)

        sums.append(lax.fori_loop(1, vols, add, part_in[sg, 0].astype(F32), unroll=True))
    total = jnp.concatenate(sums, axis=0)
    r = lax.broadcasted_iota(jnp.int32, (32, 128), 0)
    b = core * 128 + ((r % 16) // 2 * 2 + 1 - r // 16) * 8 + z
    scale = (b + 1).astype(F32) * (1.0 / math.sqrt(32768.0) / NF)
    total = total * jnp.where(r % 2 == 0, -scale, scale)
    upper = total.astype(BF)
    lower = (total - upper.astype(F32)).astype(BF)
    slots = jnp.dot(chosen, upper, preferred_element_type=F32)
    slots = slots + jnp.dot(chosen, lower, preferred_element_type=F32)
    for m in range(nars):
        slot_out[m] = slots[8 * m : 8 * m + 8]
    own_slot = pltpu.make_async_copy(slot_out.at[n], slot_in.at[n], slot_sems.at[1])
    own_slot.start()

    def send_slot(k, carry):
        m = (n + k) % nars
        pltpu.make_async_remote_copy(
            src_ref=slot_out.at[m],
            dst_ref=slot_in.at[n],
            send_sem=slot_sems.at[0],
            recv_sem=slot_sems.at[1],
            device_id={"nar": m},
            device_id_type=MESH,
        ).start()
        return carry

    lax.fori_loop(1, nars, send_slot, 0)
    pltpu.make_async_copy(slot_in, slot_in, slot_sems.at[1]).wait()
    tile = slot_in[0]
    for m in range(1, nars):
        tile = tile + slot_in[m]

    residue = (z - own_begin + NF) % 8
    for zt in range(8):
        held = jnp.where(residue == zt, 1.0, 0.0) * tile
        for xt in range(4):
            last_out[zt * 4 + xt] = held[2 * xt : 2 * xt + 2]
    own_last = pltpu.make_async_copy(last_out.at[z * 4 + x], last_in.at[z * 4 + x], last_sems.at[1])
    own_last.start()

    def send_last(k, carry):
        ut = (u + k) % vols
        pltpu.make_async_remote_copy(
            src_ref=last_out.at[(ut % 8) * 4 + ut // 8],
            dst_ref=last_in.at[z * 4 + x],
            send_sem=last_sems.at[0],
            recv_sem=last_sems.at[1],
            device_id={"vol": ut},
            device_id_type=MESH,
        ).start()
        return carry

    lax.fori_loop(1, vols, send_last, 0)
    pltpu.make_async_copy(last_in, last_in, last_sems.at[1]).wait()
    for xt in range(4):
        chunk = last_in[xt]
        for zt in range(1, 8):
            chunk = chunk + last_in[zt * 4 + xt]
        out_ref[xt] = chunk

    sent = part_out.at[pl.ds(0, 62)]
    pltpu.make_async_copy(sent, sent, part_sems.at[0]).wait()
    sent = slot_out.at[pl.ds(0, 15)]
    pltpu.make_async_copy(sent, sent, slot_sems.at[0]).wait()
    sent = last_out.at[pl.ds(0, 31)]
    pltpu.make_async_copy(sent, sent, last_sems.at[0]).wait()


def per_device(series, send_rows, bin_counts, observer_cells):
    in_vmem = pl.BlockSpec(memory_space=pltpu.VMEM)
    chunks = pl.pallas_call(
        kernel,
        out_shape=jax.ShapeDtypeStruct((4, 2, 128), F32),
        in_specs=[pl.BlockSpec(memory_space=pltpu.SMEM)] + [in_vmem] * 4,
        out_specs=in_vmem,
        scratch_shapes=[
            pltpu.VMEM((2048, 128), F32),
            pltpu.VMEM((1024, 128), F32),
            pltpu.VMEM((1024, 128), BF),
            pltpu.VMEM((1024, 128), BF),
            pltpu.VMEM((3, 128, 128), F32),
            pltpu.VMEM((3, 8, OBS), F32),
            pltpu.VMEM((8, OBS), F32),
            pltpu.VMEM((32, 128, OBS), BF),
            pltpu.VMEM((8, 8, 16, 512), BF),
            pltpu.VMEM((2, 16, OBS), F32),
            pltpu.VMEM((64, 16, 128), BF),
            pltpu.VMEM((2, 32, 16, 128), BF),
            pltpu.VMEM((16, 8, 128), F32),
            pltpu.VMEM((16, 8, 128), F32),
            pltpu.VMEM((32, 2, 128), F32),
            pltpu.VMEM((32, 2, 128), F32),
            pltpu.SemaphoreType.DMA((2,)),
            pltpu.SemaphoreType.DMA((2,)),
            pltpu.SemaphoreType.DMA((2,)),
            pltpu.SemaphoreType.DMA((2,)),
        ],
        compiler_params=pltpu.CompilerParams(
            collective_id=0, has_side_effects=True, vmem_limit_bytes=48 << 20
        ),
    )(
        bin_counts,
        series,
        send_rows.reshape(1, -1),
        observer_cells,
        jnp.asarray(dft_rows()),
    )
    return chunks.transpose(1, 0, 2).reshape(1, 1, 2, OBS)


def solution(mesh):
    placed = (P(("vol", "nar"), None), P("vol", "nar", None), P(), P())
    return jax.shard_map(
        per_device,
        mesh=mesh,
        in_specs=placed,
        out_specs=P("nar", "vol", None, None),
        check_vma=False,
    )
```

```python
import math

import jax
import jax.numpy as jnp
import ml_dtypes
import numpy as np
from jax import lax
from jax.experimental import pallas as pl
from jax.experimental.pallas import tpu as pltpu
from jax.sharding import PartitionSpec as P

NT = 512
NF = 256
NQ = 4
OBS = 512
WAVE_STEP = 0.05
BF = jnp.bfloat16
F32 = jnp.float32
MESH = pl.DeviceIdType.MESH


def dft_rows():
    steps = np.arange(NT, dtype=np.int64)
    turns = (np.arange(1, NF + 1, dtype=np.int64)[:, None] * steps[None, :]) % NT
    angle = turns.astype(np.float32) * np.float32(2.0 * math.pi / NT)
    table = np.stack([np.cos(angle), -np.sin(angle)], axis=1)
    return table.reshape(2 * NF, NT).astype(ml_dtypes.bfloat16)


SIN_TERMS = [(-1.0) ** i / math.factorial(2 * i + 1) for i in range(7)]
COS_TERMS = [(-1.0) ** i / math.factorial(2 * i) for i in range(8)]


def polynomial(terms, square):
    total = terms[-1]
    for term in terms[-2::-1]:
        total = total * square + term
    return total


def cos_sin(turns):
    half = (turns - jnp.round(turns)) * math.pi
    square = half * half
    s = half * polynomial(SIN_TERMS, square)
    c = polynomial(COS_TERMS, square)
    return 1.0 - 2.0 * s * s, 2.0 * s * c


def times(one, other):
    return one[0] * other[0] - one[1] * other[1], one[0] * other[1] + one[1] * other[0]


def squared(one):
    return 1.0 - 2.0 * one[1] * one[1], 2.0 * one[0] * one[1]


def modulo(value, base):
    rest = value - (value.astype(F32) * (1.0 / base)).astype(jnp.int32) * base
    rest = jnp.where(rest < 0, rest + base, rest)
    return jnp.where(rest >= base, rest - base, rest)


def kernel(
    counts_hbm,
    series_hbm,
    listing_hbm,
    cells_hbm,
    dft_hbm,
    out_ref,
    counts_ref,
    series_ref,
    listing_ref,
    cells_ref,
    dft_ref,
    spec,
    own,
    swap_out,
    swap_in,
    place,
    facing,
    weight,
    table,
    coef,
    stage,
    part_out,
    part_in,
    slot_out,
    slot_in,
    last_out,
    last_in,
    swap_sems,
    sent_sem,
    part_sems,
    slot_sems,
    last_sems,
    load_sems,
):
    u = lax.axis_index("vol")
    n = lax.axis_index("nar")
    x, z = u // 8, u % 8
    core = n % 2
    vols, nars = 32, 16

    loads = [
        pltpu.make_async_copy(source, target, load_sems.at[i])
        for i, (source, target) in enumerate(
            (
                (dft_hbm, dft_ref),
                (series_hbm, series_ref),
                (listing_hbm, listing_ref),
                (cells_hbm, cells_ref),
                (counts_hbm, counts_ref),
            )
        )
    ]
    for load in loads:
        load.start()

    barrier = pltpu.get_barrier_semaphore()

    def greet_vol(k, carry):
        pl.semaphore_signal(barrier, inc=1, device_id={"vol": (u + k) % vols}, device_id_type=MESH)
        return carry

    def greet_nar(k, carry):
        pl.semaphore_signal(barrier, inc=1, device_id={"nar": (n + k) % nars}, device_id_type=MESH)
        return carry

    lax.fori_loop(1, vols, greet_vol, 0)
    lax.fori_loop(1, nars, greet_nar, 0)
    for load in loads:
        load.wait()

    pick = lax.broadcasted_iota(jnp.int32, (64, 64), 0) == listing_ref[...]
    surface = lax.dot_general(
        jnp.where(pick, 1.0, 0.0).astype(BF),
        series_ref[...],
        (((0,), (0,)), ((), ())),
        preferred_element_type=F32,
    ).astype(BF)
    rows = jnp.concatenate([surface[:, q * NT : (q + 1) * NT] for q in range(NQ)], axis=0)

    def transform(half):
        lines = dft_ref[pl.ds(pl.multiple_of(half * 256, 256), 256), :]
        spectra = lax.dot_general(lines, rows, (((1,), (1,)), ((), ())), preferred_element_type=F32)
        spectra = spectra * (1.0 / math.sqrt(NT))
        for q in range(NQ):
            both = spectra[:, q // 2 * 128 : q // 2 * 128 + 128]
            spec[pl.ds(q, 256, stride=NQ), :] = jnp.where(core == q % 2, both, pltpu.roll(both, 64, 1))

    transform(1 - core)
    swap_out[...] = spec[...].astype(BF)
    pl.semaphore_wait(barrier, vols + nars - 2)
    swap = pltpu.make_async_remote_copy(
        src_ref=swap_out,
        dst_ref=swap_in,
        send_sem=swap_sems.at[0],
        recv_sem=swap_sems.at[1],
        device_id={"nar": n + 1 - 2 * core},
        device_id_type=MESH,
    )
    swap.start()
    transform(core)

    slab = u * 8 + n // 2
    point = slab * 128 + lax.broadcasted_iota(jnp.int32, (128, 128), 0)
    c, s = cos_sin(modulo(point * 1597, 8191).astype(F32) * (1.0 / 8191.0))
    place[0] = 20.0 * c
    place[1] = 20.0 * s
    place[2] = slab.astype(F32) * 0.5 + modulo(point * 613, 127).astype(F32) * (0.37 / 127.0)
    cells = cells_ref[...].astype(F32)
    polar = cos_sin((cells[0:1] + 0.5) * (1.0 / 256.0))
    azimuth = cos_sin(cells[1:2] * (1.0 / 128.0))
    facing[0] = jnp.broadcast_to(polar[1] * azimuth[0], (8, OBS))
    facing[1] = jnp.broadcast_to(polar[1] * azimuth[1], (8, OBS))
    facing[2] = jnp.broadcast_to(polar[0], (8, OBS))
    term = lax.broadcasted_iota(jnp.int32, (8, OBS), 0) % NQ
    weight[...] = jnp.where(
        term == 0,
        1.0,
        jnp.where(term == 1, facing[0], jnp.where(term == 2, facing[1], facing[2])),
    )

    def fill(at, carry):
        rows16 = pl.ds(pl.multiple_of((at // 2) * 16, 16), 16)
        lanes = pl.ds(pl.multiple_of((at % 2) * 256, 256), 256)
        dotted = 0.0
        for axis in range(3):
            spot = place[axis, rows16, :]
            look = facing[axis, :, lanes]
            dotted = dotted + jnp.concatenate([spot, spot], axis=1) * jnp.concatenate([look, look], axis=0)
        turns = dotted * (WAVE_STEP / (2.0 * math.pi))

        def keep(index, value):
            table[index, rows16, lanes] = value[0].astype(BF)
            table[index + 1, rows16, lanes] = value[1].astype(BF)

        step = cos_sin(turns)
        coarse = cos_sin(turns * (core.astype(F32) * 128.0 + 61.0))
        keep(0, coarse)
        for r in range(1, 8):
            coarse = times(coarse, step)
            keep(2 * r, coarse)
        fine = squared(squared(step))
        step = squared(fine)
        keep(16, fine)
        for j in range(1, 8):
            fine = times(fine, step)
            keep(16 + 2 * j, fine)
        return carry

    lax.fori_loop(0, 16, fill, 0)

    swap.wait()
    held_here = lax.broadcasted_iota(jnp.int32, (64, 128), 1) // 64 == core

    def join(at, carry):
        here = pl.ds(pl.multiple_of(at * 64, 64), 64)
        own[here, :] = jnp.where(held_here, spec[here, :], swap_in[here, :].astype(F32))
        return carry

    lax.fori_loop(0, 16, join, 0)
    sign = jnp.where(lax.broadcasted_iota(jnp.int32, (8, 128), 0) < 4, 1.0, -1.0)

    def lay(r, carry):
        for j in range(8):
            high = own[pl.ds(pl.multiple_of((r + 8 * (8 + j)) * 8, 8), 8), :]
            low = own[pl.ds(pl.multiple_of((r + 8 * (7 - j)) * 8, 8), 8), :]
            high2 = pltpu.roll(high, 4, 0) * sign
            low2 = pltpu.roll(low, 4, 0) * sign
            blocks = ((high, low), (-high, low), (high2, low2), (high2, -low2))
            for k, both in enumerate(blocks):
                coef[r, j, :, pl.ds(k * 128, 128)] = jnp.concatenate(both, axis=0).astype(BF)
        return carry

    lax.fori_loop(0, 8, lay, 0)

    def one_plane(step, carry):
        zt = (z + 4 + (1 - 2 * (step % 2)) * ((step + 1) // 2)) % 8
        for part in range(2):
            half = (x // 2 + 1 + part) % 2
            lanes = pl.ds(pl.multiple_of(half * 256, 256), 256)
            for j in range(8):
                c, s = table[2 * zt, :, lanes], table[2 * zt + 1, :, lanes]
                fc, fs = table[16 + 2 * j, :, lanes], table[17 + 2 * j, :, lanes]
                green = jnp.concatenate([c * fc, s * fs, s * fc, c * fs], axis=0)
                sums = jnp.dot(coef[zt, j], green, preferred_element_type=F32)
                for sg, k in enumerate((8 + j, 7 - j)):
                    total = sums[8 * sg : 8 * sg + 8] * weight[:, lanes]
                    total = total + pltpu.roll(total, 7, 0)
                    total = total + pltpu.roll(total, 6, 0)
                    stage[part, 2 * k : 2 * k + 1, :] = total[4:5]
                    stage[part, 2 * k + 1 : 2 * k + 2, :] = total[0:1]
            for k in range(2):
                xt = 2 * half + (x + 1 + k) % 2
                chosen = jnp.where((x + 1 + k) % 2 == 0, stage[part, :, 0:128], stage[part, :, 128:256])
                part_out[step * 4 + xt] = chosen.astype(BF)

                def send(xt=xt):
                    pltpu.make_async_remote_copy(
                        src_ref=part_out.at[step * 4 + xt],
                        dst_ref=part_in.at[step * 4 + x],
                        send_sem=sent_sem.at[0],
                        recv_sem=part_sems.at[step],
                        device_id={"vol": xt * 8 + zt},
                        device_id_type=MESH,
                    ).start()

                if part == 1 and k == 1:
                    pl.when(step < 7)(send)
                else:
                    send()
        return carry

    lax.fori_loop(0, 8, one_plane, 0)
    part_in[28 + x] = part_out[28 + x]

    row = lax.broadcasted_iota(jnp.int32, (128, 32), 0)
    col = lax.broadcasted_iota(jnp.int32, (128, 32), 1)
    bin_of = core * 128 + col // 2 * 8 + z
    begin, begins, counts = jnp.int32(0), jnp.zeros_like(row), jnp.zeros_like(row)
    own_begin = jnp.int32(0)
    for m in range(nars):
        amount = counts_ref[m]
        begins = jnp.where(row // 8 == m, begin, begins)
        counts = jnp.where(row // 8 == m, amount, counts)
        own_begin = own_begin + jnp.where(m < n, amount, 0)
        begin = begin + amount
    seat = bin_of - begins
    ahead = seat - (row % 8) // 2 * 8
    chosen = (row % 2 == col % 2) & (ahead >= 0) & (ahead < 8) & (seat < counts)
    chosen = jnp.where(chosen, 1.0, 0.0).astype(BF)

    total = jnp.zeros((32, 128), F32)
    for step in range(8):
        arrived = part_in.at[pl.ds(step * 4, 4 if step < 7 else 3)]
        pltpu.make_async_copy(arrived, arrived, part_sems.at[step]).wait()
        for xs in range(4):
            total = total + part_in[step * 4 + xs].astype(F32)
    r = lax.broadcasted_iota(jnp.int32, (32, 128), 0)
    b = core * 128 + r // 2 * 8 + z
    scale = (b + 1).astype(F32) * (1.0 / math.sqrt(32768.0) / NF)
    total = total * jnp.where(r % 2 == 0, -scale, scale)
    upper = total.astype(BF)
    lower = (total - upper.astype(F32)).astype(BF)
    slots = jnp.dot(chosen, upper, preferred_element_type=F32)
    slots = slots + jnp.dot(chosen, lower, preferred_element_type=F32)
    for m in range(nars):
        slot_out[m] = slots[8 * m : 8 * m + 8]
    own_slot = pltpu.make_async_copy(slot_out.at[n], slot_in.at[n], slot_sems.at[1])
    own_slot.start()

    def send_slot(at, carry):
        m = (n + 8 + (1 - 2 * (at % 2)) * ((at + 1) // 2)) % nars
        pltpu.make_async_remote_copy(
            src_ref=slot_out.at[m],
            dst_ref=slot_in.at[n],
            send_sem=slot_sems.at[0],
            recv_sem=slot_sems.at[1],
            device_id={"nar": m},
            device_id_type=MESH,
        ).start()
        return carry

    lax.fori_loop(0, nars - 1, send_slot, 0)
    pltpu.make_async_copy(slot_in, slot_in, slot_sems.at[1]).wait()
    tile = slot_in[0]
    for m in range(1, nars):
        tile = tile + slot_in[m]

    residue = (z - own_begin + NF) % 8
    for zt in range(8):
        held = jnp.where(residue == zt, 1.0, 0.0) * tile
        for xt in range(4):
            last_out[zt * 4 + xt] = held[2 * xt : 2 * xt + 2]
    own_last = pltpu.make_async_copy(last_out.at[z * 4 + x], last_in.at[z * 4 + x], last_sems.at[1])
    own_last.start()

    away = [(kx, kz) for kx in range(4) for kz in range(8) if kx or kz]
    for kx, kz in sorted(away, key=lambda k: -min(k[0], 4 - k[0]) - min(k[1], 8 - k[1])):
        xt, zt = (x + kx) % 4, (z + kz) % 8
        pltpu.make_async_remote_copy(
            src_ref=last_out.at[zt * 4 + xt],
            dst_ref=last_in.at[z * 4 + x],
            send_sem=last_sems.at[0],
            recv_sem=last_sems.at[1],
            device_id={"vol": xt * 8 + zt},
            device_id_type=MESH,
        ).start()
    pltpu.make_async_copy(last_in, last_in, last_sems.at[1]).wait()
    for xt in range(4):
        chunk = last_in[xt]
        for zt in range(1, 8):
            chunk = chunk + last_in[zt * 4 + xt]
        out_ref[xt] = chunk

    sent = part_out.at[pl.ds(0, 31)]
    pltpu.make_async_copy(sent, sent, sent_sem.at[0]).wait()
    sent = slot_out.at[pl.ds(0, 15)]
    pltpu.make_async_copy(sent, sent, slot_sems.at[0]).wait()
    sent = last_out.at[pl.ds(0, 31)]
    pltpu.make_async_copy(sent, sent, last_sems.at[0]).wait()


def per_device(series, send_rows, bin_counts, observer_cells):
    in_vmem = pl.BlockSpec(memory_space=pltpu.VMEM)
    chunks = pl.pallas_call(
        kernel,
        out_shape=jax.ShapeDtypeStruct((4, 2, 128), F32),
        in_specs=[pl.BlockSpec(memory_space=pl.ANY)] * 5,
        out_specs=in_vmem,
        scratch_shapes=[
            pltpu.SMEM((16,), jnp.int32),
            pltpu.VMEM((64, NQ * NT), BF),
            pltpu.VMEM((1, 64), jnp.int32),
            pltpu.VMEM((2, OBS), jnp.int32),
            pltpu.VMEM((2 * NF, NT), BF),
            pltpu.VMEM((1024, 128), F32),
            pltpu.VMEM((1024, 128), F32),
            pltpu.VMEM((1024, 128), BF),
            pltpu.VMEM((1024, 128), BF),
            pltpu.VMEM((3, 128, 128), F32),
            pltpu.VMEM((3, 8, OBS), F32),
            pltpu.VMEM((8, OBS), F32),
            pltpu.VMEM((32, 128, OBS), BF),
            pltpu.VMEM((8, 8, 16, 512), BF),
            pltpu.VMEM((2, 32, 256), F32),
            pltpu.VMEM((32, 32, 128), BF),
            pltpu.VMEM((32, 32, 128), BF),
            pltpu.VMEM((16, 8, 128), F32),
            pltpu.VMEM((16, 8, 128), F32),
            pltpu.VMEM((32, 2, 128), F32),
            pltpu.VMEM((32, 2, 128), F32),
            pltpu.SemaphoreType.DMA((2,)),
            pltpu.SemaphoreType.DMA((1,)),
            pltpu.SemaphoreType.DMA((8,)),
            pltpu.SemaphoreType.DMA((2,)),
            pltpu.SemaphoreType.DMA((2,)),
            pltpu.SemaphoreType.DMA((5,)),
        ],
        compiler_params=pltpu.CompilerParams(
            collective_id=0, has_side_effects=True, vmem_limit_bytes=56 << 20
        ),
    )(
        bin_counts,
        series,
        send_rows.reshape(1, -1),
        observer_cells,
        jnp.asarray(dft_rows()),
    )
    return chunks.transpose(1, 0, 2).reshape(1, 1, 2, OBS)


def solution(mesh):
    placed = (P(("vol", "nar"), None), P("vol", "nar", None), P(), P())
    return jax.shard_map(
        per_device,
        mesh=mesh,
        in_specs=placed,
        out_specs=P("nar", "vol", None, None),
        check_vma=False,
    )
```

```python
import math

import jax
import jax.numpy as jnp
import ml_dtypes
import numpy as np
from jax import lax
from jax.experimental import pallas as pl
from jax.experimental.pallas import tpu as pltpu
from jax.sharding import PartitionSpec as P

NT = 512
NF = 256
NQ = 4
OBS = 512
WAVE_STEP = 0.05
BF = jnp.bfloat16
F32 = jnp.float32
MESH = pl.DeviceIdType.MESH


def dft_rows():
    steps = np.arange(NT, dtype=np.int64)
    turns = (np.arange(1, NF + 1, dtype=np.int64)[:, None] * steps[None, :]) % NT
    angle = turns.astype(np.float32) * np.float32(2.0 * math.pi / NT)
    table = np.stack([np.cos(angle), -np.sin(angle)], axis=1)
    return table.reshape(2 * NF, NT).astype(ml_dtypes.bfloat16)


SIN_TERMS = [(-1.0) ** i / math.factorial(2 * i + 1) for i in range(6)]
COS_TERMS = [(-1.0) ** i / math.factorial(2 * i) for i in range(7)]


def polynomial(terms, square):
    total = terms[-1]
    for term in terms[-2::-1]:
        total = total * square + term
    return total


def cos_sin(turns):
    half = (turns - jnp.round(turns)) * math.pi
    square = half * half
    s = half * polynomial(SIN_TERMS, square)
    c = polynomial(COS_TERMS, square)
    return 1.0 - 2.0 * s * s, 2.0 * s * c


def times(one, other):
    return one[0] * other[0] - one[1] * other[1], one[0] * other[1] + one[1] * other[0]


def squared(one):
    return 1.0 - 2.0 * one[1] * one[1], 2.0 * one[0] * one[1]


def modulo(value, base):
    rest = value - (value.astype(F32) * (1.0 / base)).astype(jnp.int32) * base
    rest = jnp.where(rest < 0, rest + base, rest)
    return jnp.where(rest >= base, rest - base, rest)


def kernel(
    counts_hbm,
    series_hbm,
    listing_hbm,
    cells_hbm,
    dft_hbm,
    out_ref,
    counts_ref,
    series_ref,
    listing_ref,
    cells_ref,
    dft_ref,
    spec,
    swap_out,
    swap_in,
    place,
    facing,
    weight,
    table,
    coef,
    begun,
    picks,
    scale,
    stage,
    part_out,
    part_in,
    relay_out,
    relay_in,
    slot_out,
    slot_in,
    tile,
    last_out,
    last_in,
    swap_sems,
    sent_sem,
    part_sems,
    relay_sems,
    slot_sems,
    last_sems,
    load_sems,
):
    u = lax.axis_index("vol")
    n = lax.axis_index("nar")
    x, z = u // 8, u % 8
    core = n % 2
    y = n // 2
    nars = 16

    loads = [
        pltpu.make_async_copy(source, target, load_sems.at[i])
        for i, (source, target) in enumerate(
            (
                (cells_hbm, cells_ref),
                (counts_hbm, counts_ref),
                (listing_hbm, listing_ref),
                (series_hbm, series_ref),
                (dft_hbm, dft_ref),
            )
        )
    ]
    for load in loads:
        load.start()

    barrier = pltpu.get_barrier_semaphore()

    by_xz = [(a, b) for a in range(4) for b in range(8) if a or b]
    by_xz.sort(key=lambda k: -min(k[0], 4 - k[0]) - min(k[1], 8 - k[1]))
    by_zc = [(a, b) for a in range(8) for b in range(2) if a or b]
    by_zc.sort(key=lambda k: -min(k[0], 8 - k[0]) - k[1])

    def at_xz(a, b):
        return {"vol": (x + a) % 4 * 8 + (z + b) % 8}

    def at_xy(a, b):
        return {"vol": (x + a) % 4 * 8 + z, "nar": (y + b) % 8 * 2 + core}

    def at_zc(a, b):
        return {"vol": x * 8 + (z + a) % 8, "nar": y * 2 + (core + b) % 2}

    met = [(*k, 0, 0) for k in by_xz]
    met += [(k[0], 0, k[1], 0) for k in by_xz if k[1]]
    met += [(0, k[0], 0, k[1]) for k in by_zc if k[1]]
    met.sort(key=lambda k: -min(k[0], 4 - k[0]) - min(k[1], 8 - k[1]) - min(k[2], 8 - k[2]))
    for a, b, c, d in met:
        other = {
            "vol": (x + a) % 4 * 8 + (z + b) % 8,
            "nar": (y + c) % 8 * 2 + (core + d) % 2,
        }
        pl.semaphore_signal(barrier, inc=1, device_id=other, device_id_type=MESH)

    loads[0].wait()
    slab = u * 8 + n // 2
    point = slab * 128 + (lax.broadcasted_iota(jnp.int32, (128, 128), 0) + 64 * core) % 128
    c, s = cos_sin(modulo(point * 1597, 8191).astype(F32) * (1.0 / 8191.0))
    place[0] = 20.0 * c
    place[1] = 20.0 * s
    place[2] = slab.astype(F32) * 0.5 + modulo(point * 613, 127).astype(F32) * (0.37 / 127.0)
    cells = cells_ref[...].astype(F32)
    polar = cos_sin((cells[0:1] + 0.5) * (1.0 / 256.0))
    azimuth = cos_sin(cells[1:2] * (1.0 / 128.0))
    facing[0] = jnp.broadcast_to(polar[1] * azimuth[0], (8, OBS))
    facing[1] = jnp.broadcast_to(polar[1] * azimuth[1], (8, OBS))
    facing[2] = jnp.broadcast_to(polar[0], (8, OBS))
    term = lax.broadcasted_iota(jnp.int32, (8, OBS), 0) % NQ
    weight[...] = jnp.where(
        term == 0,
        1.0,
        jnp.where(term == 1, facing[0], jnp.where(term == 2, facing[1], facing[2])),
    )

    def fill(at, carry):
        rows16 = pl.ds(pl.multiple_of((at // 2) * 16, 16), 16)
        lanes = pl.ds(pl.multiple_of((at % 2) * 256, 256), 256)
        dotted = 0.0
        for axis in range(3):
            spot = place[axis, rows16, :]
            look = facing[axis, :, lanes]
            dotted = dotted + jnp.concatenate([spot, spot], axis=1) * jnp.concatenate([look, look], axis=0)
        turns = dotted * (WAVE_STEP / (2.0 * math.pi))

        def keep(index, value):
            table[index, rows16, lanes] = value[0].astype(BF)
            table[index + 1, rows16, lanes] = value[1].astype(BF)

        def onward(index, before, now, step):
            twice = 2.0 * step[0]
            keep(index, now)
            for k in range(1, 8):
                after = twice * now[0] - before[0], twice * now[1] - before[1]
                before, now = now, after
                keep(index + 2 * k, now)

        step = cos_sin(turns)
        coarse = cos_sin(turns * (core.astype(F32) * 128.0 + 61.0))
        onward(0, times(coarse, (step[0], -step[1])), coarse, step)
        fine = squared(squared(step))
        onward(16, (fine[0], -fine[1]), fine, squared(fine))
        return carry

    lax.fori_loop(0, 16, fill, 0)

    loads[1].wait()
    row = lax.broadcasted_iota(jnp.int32, (128, 32), 0)
    col = lax.broadcasted_iota(jnp.int32, (128, 32), 1)
    bin_of = core * 128 + col // 2 * 8 + z
    owner = row // 16 * 2 + row % 4 // 2
    begin, begins, counts = jnp.int32(0), jnp.zeros_like(row), jnp.zeros_like(row)
    own_begins = [jnp.int32(0), jnp.int32(0)]
    for m in range(nars):
        amount = counts_ref[m]
        begins = jnp.where(owner == m, begin, begins)
        counts = jnp.where(owner == m, amount, counts)
        for k in range(2):
            own_begins[k] = own_begins[k] + jnp.where(m < 2 * y + k, amount, 0)
        begin = begin + amount
    seat = bin_of - begins
    ahead = seat - row // 4 % 4 * 8
    chosen = (row % 2 == col % 2) & (ahead >= 0) & (ahead < 8) & (seat < counts)
    picks[...] = jnp.where(chosen, 1.0, 0.0).astype(BF)
    r = lax.broadcasted_iota(jnp.int32, (32, 128), 0)
    b = core * 128 + r // 2 * 8 + z
    amount = (b + 1).astype(F32) * (1.0 / math.sqrt(32768.0) / NF)
    scale[...] = jnp.where(r % 2 == 0, -amount, amount)

    for load in loads[2:]:
        load.wait()
    pick = lax.broadcasted_iota(jnp.int32, (64, 64), 0) == listing_ref[...]
    surface = lax.dot_general(
        jnp.where(pick, 1.0, 0.0).astype(BF),
        series_ref[...],
        (((0,), (0,)), ((), ())),
        preferred_element_type=F32,
    ).astype(BF)
    rows = jnp.concatenate([surface[:, q * NT : (q + 1) * NT] for q in range(NQ)], axis=0)

    def transform(half):
        lines = dft_ref[pl.ds(pl.multiple_of(half * 256, 256), 256), :]
        spectra = lax.dot_general(lines, rows, (((1,), (1,)), ((), ())), preferred_element_type=F32)
        spectra = spectra * (1.0 / math.sqrt(NT))
        first = lax.broadcasted_iota(jnp.int32, (256, 128), 1) < 64
        for q in range(NQ):
            both = spectra[:, q // 2 * 128 : q // 2 * 128 + 128]
            flipped = pltpu.roll(both, 64, 1)
            twice = jnp.where(first, flipped, both) if q % 2 else jnp.where(first, both, flipped)
            spec[pl.ds(q, 256, stride=NQ), :] = twice

    transform(1 - core)
    swap_out[...] = spec[...].astype(BF)
    transform(core)

    sign = jnp.where(lax.broadcasted_iota(jnp.int32, (8, 128), 0) < 4, 1.0, -1.0)
    turn = jnp.where(lax.broadcasted_iota(jnp.int32, (8, 128), 1) < 64, 1.0, -1.0)

    def lay_at(lane):
        def lay(r, carry):
            for j in range(8):
                high = spec[pl.ds(pl.multiple_of((r + 8 * (8 + j)) * 8, 8), 8), :]
                low = spec[pl.ds(pl.multiple_of((r + 8 * (7 - j)) * 8, 8), 8), :]
                high2 = pltpu.roll(high, 4, 0) * sign
                low2 = pltpu.roll(low, 4, 0) * sign
                blocks = ((high * turn, low), (high2, low2 * turn))
                for k, both in enumerate(blocks):
                    lanes = pl.ds(lane + k * 128, 128)
                    coef[r, j, :, lanes] = jnp.concatenate(both, axis=0).astype(BF)
            return carry

        lax.fori_loop(0, 8, lay, 0)

    def plane_of(step):
        return (z + 4 + (1 - 2 * (step % 2)) * ((step + 1) // 2)) % 8

    def products(zt, j, lanes, first, last):
        green = []
        for block in range(first, last):
            points = pl.ds(block * 64, 64)
            c, s = table[2 * zt, points, lanes], table[2 * zt + 1, points, lanes]
            fc, fs = table[16 + 2 * j, points, lanes], table[17 + 2 * j, points, lanes]
            green += [c * fc, s * fs, s * fc, c * fs]
        left = coef[zt, j, :, pl.ds(first * 256, (last - first) * 256)]
        return jnp.dot(left, jnp.concatenate(green, axis=0), preferred_element_type=F32)

    def begin_plane(step, carry):
        zt = plane_of(step)
        for half in range(2):
            lanes = pl.ds(half * 256, 256)
            for j in range(8):
                begun[step, j, :, lanes] = products(zt, j, lanes, 0, 1)
        return carry

    def finish_plane(step, carry, first, relayed=False):
        zt = plane_of(step)
        for part in range(2):
            half = (x // 2 + 1 + part) % 2
            lanes = pl.ds(pl.multiple_of(half * 256, 256), 256)
            for j in range(8):
                sums = products(zt, j, lanes, first, 2)
                if first:
                    sums = sums + begun[step, j, :, lanes]
                for sg, k in enumerate((8 + j, 7 - j)):
                    total = sums[8 * sg : 8 * sg + 8] * weight[:, lanes]
                    total = total + pltpu.roll(total, 7, 0)
                    total = total + pltpu.roll(total, 6, 0)
                    stage[part, 2 * k : 2 * k + 1, :] = total[4:5]
                    stage[part, 2 * k + 1 : 2 * k + 2, :] = total[0:1]
            for k in range(2):
                xt = 2 * half + (x + 1 + k) % 2
                chosen = jnp.where((x + 1 + k) % 2 == 0, stage[part, :, 0:128], stage[part, :, 128:256])
                part_out[step * 4 + xt] = chosen.astype(BF)

                def send(xt=xt):
                    pltpu.make_async_remote_copy(
                        src_ref=part_out.at[step * 4 + xt],
                        dst_ref=(relay_in if relayed else part_in).at[step * 4 + x],
                        send_sem=sent_sem.at[0],
                        recv_sem=(relay_sems if relayed else part_sems).at[step],
                        device_id={"vol": xt * 8 + (z if relayed else zt)},
                        device_id_type=MESH,
                    ).start()

                if part == 1 and k == 1:
                    if not relayed:
                        pl.when(step < 7)(send)
                else:
                    send()
        return carry

    def relay(step):
        arrived = relay_in.at[pl.ds(step * 4, 3)]
        pltpu.make_async_copy(arrived, arrived, relay_sems.at[step]).wait()
        relay_in[step * 4 + x] = part_out[step * 4 + x]
        total = relay_in[step * 4].astype(F32)
        for xs in range(1, 4):
            total = total + relay_in[step * 4 + xs].astype(F32)
        relay_out[step] = total.astype(BF)
        pltpu.make_async_remote_copy(
            src_ref=relay_out.at[step],
            dst_ref=part_in.at[step * 4],
            send_sem=sent_sem.at[0],
            recv_sem=part_sems.at[step],
            device_id={"vol": x * 8 + plane_of(step)},
            device_id_type=MESH,
        ).start()

    lay_at(0)
    lax.fori_loop(0, 2, begin_plane, 0)
    pl.semaphore_wait(barrier, len(met))
    swap = pltpu.make_async_remote_copy(
        src_ref=swap_out,
        dst_ref=swap_in,
        send_sem=swap_sems.at[0],
        recv_sem=swap_sems.at[1],
        device_id=at_zc(0, 1),
        device_id_type=MESH,
    )
    swap.start()
    lax.fori_loop(2, 6, begin_plane, 0)
    swap.wait()
    spec[...] = swap_in[...].astype(F32)
    lay_at(256)
    lax.fori_loop(0, 3, lambda step, carry: finish_plane(step, carry, 1, True), 0)
    lax.fori_loop(3, 6, lambda step, carry: finish_plane(step, carry, 1), 0)
    lax.fori_loop(6, 7, lambda step, carry: finish_plane(step, carry, 0), 0)
    relay(0)
    lax.fori_loop(7, 8, lambda step, carry: finish_plane(step, carry, 0), 0)
    relay(1)
    relay(2)
    part_in[28 + x] = part_out[28 + x]

    total = jnp.zeros((32, 128), F32)
    for step in (3, 4, 5, 6, 7, 0, 1, 2):
        tiles = 1 if step < 3 else 4
        arrived = part_in.at[pl.ds(step * 4, tiles if step < 7 else 3)]
        pltpu.make_async_copy(arrived, arrived, part_sems.at[step]).wait()
        for k in range(tiles):
            total = total + part_in[step * 4 + k].astype(F32)
    total = total * scale[...]
    chosen = picks[...]
    upper = total.astype(BF)
    lower = (total - upper.astype(F32)).astype(BF)
    slots = jnp.dot(chosen, upper, preferred_element_type=F32)
    slots = slots + jnp.dot(chosen, lower, preferred_element_type=F32)
    for k in range(32):
        slot_out[k] = slots[4 * k : 4 * k + 4]
    slot_in[y * 4 + x] = slot_out[y * 4 + x]
    for a, b in by_xz:
        pltpu.make_async_remote_copy(
            src_ref=slot_out.at[(y + b) % 8 * 4 + (x + a) % 4],
            dst_ref=slot_in.at[y * 4 + x],
            send_sem=slot_sems.at[0],
            recv_sem=slot_sems.at[1],
            device_id=at_xy(a, b),
            device_id_type=MESH,
        ).start()
    arrived = slot_in.at[pl.ds(0, 31)]
    pltpu.make_async_copy(arrived, arrived, slot_sems.at[1]).wait()
    for xs in range(4):
        chunk = slot_in[xs]
        for ys in range(1, 8):
            chunk = chunk + slot_in[ys * 4 + xs]
        for k in range(2):
            tile[k, 2 * xs : 2 * xs + 2, :] = chunk[2 * k : 2 * k + 2]

    for k in range(2):
        residue = (z - own_begins[k] + NF) % 8
        whole = tile[k]
        for zt in range(8):
            last_out[zt * 2 + k] = jnp.where(residue == zt, 1.0, 0.0) * whole
    last_in[z * 2 + core] = last_out[z * 2 + core]
    for a, b in by_zc:
        pltpu.make_async_remote_copy(
            src_ref=last_out.at[(z + a) % 8 * 2 + (core + b) % 2],
            dst_ref=last_in.at[z * 2 + core],
            send_sem=last_sems.at[0],
            recv_sem=last_sems.at[1],
            device_id=at_zc(a, b),
            device_id_type=MESH,
        ).start()
    arrived = last_in.at[pl.ds(0, 15)]
    pltpu.make_async_copy(arrived, arrived, last_sems.at[1]).wait()
    whole = last_in[0]
    for k in range(1, 16):
        whole = whole + last_in[k]
    out_ref[...] = whole

    sent = part_out.at[pl.ds(0, 31)]
    pltpu.make_async_copy(sent, sent, sent_sem.at[0]).wait()
    sent = slot_out.at[pl.ds(0, 31)]
    pltpu.make_async_copy(sent, sent, slot_sems.at[0]).wait()
    sent = last_out.at[pl.ds(0, 15)]
    pltpu.make_async_copy(sent, sent, last_sems.at[0]).wait()


def per_device(series, send_rows, bin_counts, observer_cells):
    in_vmem = pl.BlockSpec(memory_space=pltpu.VMEM)
    chunks = pl.pallas_call(
        kernel,
        out_shape=jax.ShapeDtypeStruct((8, 128), F32),
        in_specs=[pl.BlockSpec(memory_space=pl.ANY)] * 5,
        out_specs=in_vmem,
        scratch_shapes=[
            pltpu.SMEM((16,), jnp.int32),
            pltpu.VMEM((64, NQ * NT), BF),
            pltpu.VMEM((1, 64), jnp.int32),
            pltpu.VMEM((2, OBS), jnp.int32),
            pltpu.VMEM((2 * NF, NT), BF),
            pltpu.VMEM((1024, 128), F32),
            pltpu.VMEM((1024, 128), BF),
            pltpu.VMEM((1024, 128), BF),
            pltpu.VMEM((3, 128, 128), F32),
            pltpu.VMEM((3, 8, OBS), F32),
            pltpu.VMEM((8, OBS), F32),
            pltpu.VMEM((32, 128, OBS), BF),
            pltpu.VMEM((8, 8, 16, 512), BF),
            pltpu.VMEM((6, 8, 16, OBS), F32),
            pltpu.VMEM((128, 32), BF),
            pltpu.VMEM((32, 128), F32),
            pltpu.VMEM((2, 32, 256), F32),
            pltpu.VMEM((32, 32, 128), BF),
            pltpu.VMEM((32, 32, 128), BF),
            pltpu.VMEM((3, 32, 128), BF),
            pltpu.VMEM((12, 32, 128), BF),
            pltpu.VMEM((32, 4, 128), F32),
            pltpu.VMEM((32, 4, 128), F32),
            pltpu.VMEM((2, 8, 128), F32),
            pltpu.VMEM((16, 8, 128), F32),
            pltpu.VMEM((16, 8, 128), F32),
            pltpu.SemaphoreType.DMA((2,)),
            pltpu.SemaphoreType.DMA((1,)),
            pltpu.SemaphoreType.DMA((8,)),
            pltpu.SemaphoreType.DMA((3,)),
            pltpu.SemaphoreType.DMA((2,)),
            pltpu.SemaphoreType.DMA((2,)),
            pltpu.SemaphoreType.DMA((5,)),
        ],
        compiler_params=pltpu.CompilerParams(
            collective_id=0, has_side_effects=True, vmem_limit_bytes=56 << 20
        ),
    )(
        bin_counts,
        series,
        send_rows.reshape(1, -1),
        observer_cells,
        jnp.asarray(dft_rows()),
    )
    return chunks.reshape(4, 2, 128).transpose(1, 0, 2).reshape(1, 1, 2, OBS)


def solution(mesh):
    placed = (P(("vol", "nar"), None), P("vol", "nar", None), P(), P())
    return jax.shard_map(
        per_device,
        mesh=mesh,
        in_specs=placed,
        out_specs=P("nar", "vol", None, None),
        check_vma=False,
    )
```

```python
import math

import jax
import jax.numpy as jnp
import ml_dtypes
import numpy as np
from jax import lax
from jax.experimental import pallas as pl
from jax.experimental.pallas import tpu as pltpu
from jax.sharding import PartitionSpec as P

NT = 512
NF = 256
NQ = 4
OBS = 512
WAVE_STEP = 0.05
BF = jnp.bfloat16
F32 = jnp.float32
MESH = pl.DeviceIdType.MESH


def dft_rows():
    steps = np.arange(NT, dtype=np.int64)
    turns = (np.arange(1, NF + 1, dtype=np.int64)[:, None] * steps[None, :]) % NT
    angle = turns.astype(np.float32) * np.float32(2.0 * math.pi / NT)
    table = np.stack([np.cos(angle), -np.sin(angle)], axis=1)
    return table.reshape(2 * NF, NT).astype(ml_dtypes.bfloat16)


SIN_TERMS = [(-1.0) ** i / math.factorial(2 * i + 1) for i in range(6)]
COS_TERMS = [(-1.0) ** i / math.factorial(2 * i) for i in range(7)]


def polynomial(terms, square):
    total = terms[-1]
    for term in terms[-2::-1]:
        total = total * square + term
    return total


def cos_sin(turns):
    half = (turns - jnp.round(turns)) * math.pi
    square = half * half
    s = half * polynomial(SIN_TERMS, square)
    c = polynomial(COS_TERMS, square)
    return 1.0 - 2.0 * s * s, 2.0 * s * c


def times(one, other):
    return one[0] * other[0] - one[1] * other[1], one[0] * other[1] + one[1] * other[0]


def squared(one):
    return 1.0 - 2.0 * one[1] * one[1], 2.0 * one[0] * one[1]


def modulo(value, base):
    rest = value - (value.astype(F32) * (1.0 / base)).astype(jnp.int32) * base
    rest = jnp.where(rest < 0, rest + base, rest)
    return jnp.where(rest >= base, rest - base, rest)


def kernel(
    counts_hbm,
    series_hbm,
    listing_hbm,
    cells_hbm,
    dft_hbm,
    out_ref,
    counts_ref,
    series_ref,
    listing_ref,
    cells_ref,
    dft_ref,
    spec,
    swap_out,
    swap_in,
    place,
    facing,
    weight,
    table,
    coef,
    begun,
    picks,
    scale,
    stage,
    part_out,
    part_in,
    relay_out,
    relay_in,
    slot_out,
    slot_in,
    tile,
    last_out,
    last_in,
    swap_sems,
    sent_sem,
    part_sems,
    relay_sems,
    slot_sems,
    last_sems,
    load_sems,
):
    u = lax.axis_index("vol")
    n = lax.axis_index("nar")
    x, z = u // 8, u % 8
    core = n % 2
    y = n // 2
    nars = 16

    loads = [
        pltpu.make_async_copy(source, target, load_sems.at[i])
        for i, (source, target) in enumerate(
            (
                (cells_hbm, cells_ref),
                (counts_hbm, counts_ref),
                (listing_hbm, listing_ref),
                (series_hbm, series_ref),
                (dft_hbm, dft_ref),
            )
        )
    ]
    for load in loads:
        load.start()

    barrier = pltpu.get_barrier_semaphore()

    by_xz = [(a, b) for a in range(4) for b in range(8) if a or b]
    by_xz.sort(key=lambda k: -min(k[0], 4 - k[0]) - min(k[1], 8 - k[1]))
    by_zc = [(a, b) for a in range(8) for b in range(2) if a or b]
    by_zc.sort(key=lambda k: -min(k[0], 8 - k[0]) - k[1])

    def at_xz(a, b):
        return {"vol": (x + a) % 4 * 8 + (z + b) % 8}

    def at_xy(a, b):
        return {"vol": (x + a) % 4 * 8 + z, "nar": (y + b) % 8 * 2 + core}

    def at_zc(a, b):
        return {"vol": x * 8 + (z + a) % 8, "nar": y * 2 + (core + b) % 2}

    met = [(*k, 0, 0) for k in by_xz]
    met += [(k[0], 0, k[1], 0) for k in by_xz if k[1]]
    met += [(0, k[0], 0, k[1]) for k in by_zc if k[1]]
    met.sort(key=lambda k: -min(k[0], 4 - k[0]) - min(k[1], 8 - k[1]) - min(k[2], 8 - k[2]))
    for a, b, c, d in met:
        other = {
            "vol": (x + a) % 4 * 8 + (z + b) % 8,
            "nar": (y + c) % 8 * 2 + (core + d) % 2,
        }
        pl.semaphore_signal(barrier, inc=1, device_id=other, device_id_type=MESH)

    loads[0].wait()
    slab = u * 8 + n // 2
    point = slab * 128 + (lax.broadcasted_iota(jnp.int32, (128, 128), 0) + 64 * core) % 128
    c, s = cos_sin(modulo(point * 1597, 8191).astype(F32) * (1.0 / 8191.0))
    place[0] = 20.0 * c
    place[1] = 20.0 * s
    place[2] = slab.astype(F32) * 0.5 + modulo(point * 613, 127).astype(F32) * (0.37 / 127.0)
    cells = cells_ref[...].astype(F32)
    polar = cos_sin((cells[0:1] + 0.5) * (1.0 / 256.0))
    azimuth = cos_sin(cells[1:2] * (1.0 / 128.0))
    facing[0] = jnp.broadcast_to(polar[1] * azimuth[0], (8, OBS))
    facing[1] = jnp.broadcast_to(polar[1] * azimuth[1], (8, OBS))
    facing[2] = jnp.broadcast_to(polar[0], (8, OBS))
    term = lax.broadcasted_iota(jnp.int32, (8, OBS), 0) % NQ
    weight[...] = jnp.where(
        term == 0,
        1.0,
        jnp.where(term == 1, facing[0], jnp.where(term == 2, facing[1], facing[2])),
    )

    def fill(at, carry):
        rows16 = pl.ds(pl.multiple_of((at // 2) * 16, 16), 16)
        lanes = pl.ds(pl.multiple_of((at % 2) * 256, 256), 256)
        dotted = 0.0
        for axis in range(3):
            spot = place[axis, rows16, :]
            look = facing[axis, :, lanes]
            dotted = dotted + jnp.concatenate([spot, spot], axis=1) * jnp.concatenate([look, look], axis=0)
        turns = dotted * (WAVE_STEP / (2.0 * math.pi))

        def keep(index, value):
            table[index, rows16, lanes] = value[0].astype(BF)
            table[index + 1, rows16, lanes] = value[1].astype(BF)

        def onward(index, before, now, step):
            twice = 2.0 * step[0]
            keep(index, now)
            for k in range(1, 8):
                after = twice * now[0] - before[0], twice * now[1] - before[1]
                before, now = now, after
                keep(index + 2 * k, now)

        step = cos_sin(turns)
        coarse = cos_sin(turns * (core.astype(F32) * 128.0 + 61.0))
        onward(0, times(coarse, (step[0], -step[1])), coarse, step)
        fine = squared(squared(step))
        onward(16, (fine[0], -fine[1]), fine, squared(fine))
        return carry

    lax.fori_loop(0, 16, fill, 0)

    loads[1].wait()
    row = lax.broadcasted_iota(jnp.int32, (128, 32), 0)
    col = lax.broadcasted_iota(jnp.int32, (128, 32), 1)
    bin_of = core * 128 + col // 2 * 8 + z
    owner = row // 16 * 2 + row % 4 // 2
    begin, begins, counts = jnp.int32(0), jnp.zeros_like(row), jnp.zeros_like(row)
    own_begins = [jnp.int32(0), jnp.int32(0)]
    for m in range(nars):
        amount = counts_ref[m]
        begins = jnp.where(owner == m, begin, begins)
        counts = jnp.where(owner == m, amount, counts)
        for k in range(2):
            own_begins[k] = own_begins[k] + jnp.where(m < 2 * y + k, amount, 0)
        begin = begin + amount
    seat = bin_of - begins
    ahead = seat - row // 4 % 4 * 8
    chosen = (row % 2 == col % 2) & (ahead >= 0) & (ahead < 8) & (seat < counts)
    picks[...] = jnp.where(chosen, 1.0, 0.0).astype(BF)
    r = lax.broadcasted_iota(jnp.int32, (32, 128), 0)
    b = core * 128 + r // 2 * 8 + z
    amount = (b + 1).astype(F32) * (1.0 / math.sqrt(32768.0) / NF)
    scale[...] = jnp.where(r % 2 == 0, -amount, amount)

    for load in loads[2:]:
        load.wait()
    pick = lax.broadcasted_iota(jnp.int32, (64, 64), 0) == listing_ref[...]
    surface = lax.dot_general(
        jnp.where(pick, 1.0, 0.0).astype(BF),
        series_ref[...],
        (((0,), (0,)), ((), ())),
        preferred_element_type=F32,
    ).astype(BF)
    rows = jnp.concatenate([surface[:, q * NT : (q + 1) * NT] for q in range(NQ)], axis=0)

    def transform(half):
        lines = dft_ref[pl.ds(pl.multiple_of(half * 256, 256), 256), :]
        spectra = lax.dot_general(lines, rows, (((1,), (1,)), ((), ())), preferred_element_type=F32)
        spectra = spectra * (1.0 / math.sqrt(NT))
        first = lax.broadcasted_iota(jnp.int32, (256, 128), 1) < 64
        for q in range(NQ):
            both = spectra[:, q // 2 * 128 : q // 2 * 128 + 128]
            flipped = pltpu.roll(both, 64, 1)
            twice = jnp.where(first, flipped, both) if q % 2 else jnp.where(first, both, flipped)
            spec[pl.ds(q, 256, stride=NQ), :] = twice

    transform(1 - core)
    swap_out[...] = spec[...].astype(BF)
    transform(core)

    sign = jnp.where(lax.broadcasted_iota(jnp.int32, (8, 128), 0) < 4, 1.0, -1.0)
    turn = jnp.where(lax.broadcasted_iota(jnp.int32, (8, 128), 1) < 64, 1.0, -1.0)

    def lay_at(lane):
        def lay(r, carry):
            for j in range(8):
                high = spec[pl.ds(pl.multiple_of((r + 8 * (8 + j)) * 8, 8), 8), :]
                low = spec[pl.ds(pl.multiple_of((r + 8 * (7 - j)) * 8, 8), 8), :]
                high2 = pltpu.roll(high, 4, 0) * sign
                low2 = pltpu.roll(low, 4, 0) * sign
                blocks = ((high * turn, low), (high2, low2 * turn))
                for k, both in enumerate(blocks):
                    lanes = pl.ds(lane + k * 128, 128)
                    coef[r, j, :, lanes] = jnp.concatenate(both, axis=0).astype(BF)
            return carry

        lax.fori_loop(0, 8, lay, 0)

    def plane_of(step):
        return (z + 4 + (1 - 2 * (step % 2)) * ((step + 1) // 2)) % 8

    def products(zt, j, lanes, first, last):
        green = []
        for block in range(first, last):
            points = pl.ds(block * 64, 64)
            c, s = table[2 * zt, points, lanes], table[2 * zt + 1, points, lanes]
            fc, fs = table[16 + 2 * j, points, lanes], table[17 + 2 * j, points, lanes]
            green += [c * fc, s * fs, s * fc, c * fs]
        left = coef[zt, j, :, pl.ds(first * 256, (last - first) * 256)]
        return jnp.dot(left, jnp.concatenate(green, axis=0), preferred_element_type=F32)

    def begin_plane(step, carry):
        zt = plane_of(step)
        for half in range(2):
            lanes = pl.ds(half * 256, 256)
            for j in range(8):
                begun[step, j, :, lanes] = products(zt, j, lanes, 0, 1)
        return carry

    def finish_plane(step, carry, first, relayed=False):
        zt = plane_of(step)
        for part in range(2):
            half = (x // 2 + 1 + part) % 2
            lanes = pl.ds(pl.multiple_of(half * 256, 256), 256)
            for j in range(8):
                sums = products(zt, j, lanes, first, 2)
                if first:
                    sums = sums + begun[step, j, :, lanes]
                for sg, k in enumerate((8 + j, 7 - j)):
                    total = sums[8 * sg : 8 * sg + 8] * weight[:, lanes]
                    total = total + pltpu.roll(total, 7, 0)
                    total = total + pltpu.roll(total, 6, 0)
                    stage[part, 2 * k : 2 * k + 1, :] = total[4:5]
                    stage[part, 2 * k + 1 : 2 * k + 2, :] = total[0:1]
            for k in range(2):
                xt = 2 * half + (x + 1 + k) % 2
                chosen = jnp.where((x + 1 + k) % 2 == 0, stage[part, :, 0:128], stage[part, :, 128:256])
                part_out[step * 4 + xt] = chosen.astype(BF)

                def send(xt=xt):
                    pltpu.make_async_remote_copy(
                        src_ref=part_out.at[step * 4 + xt],
                        dst_ref=(relay_in if relayed else part_in).at[step * 4 + x],
                        send_sem=sent_sem.at[0],
                        recv_sem=(relay_sems if relayed else part_sems).at[step],
                        device_id={"vol": xt * 8 + (z if relayed else zt)},
                        device_id_type=MESH,
                    ).start()

                if part == 1 and k == 1:
                    if not relayed:
                        pl.when(step < 7)(send)
                else:
                    send()
        return carry

    def relay(step):
        arrived = relay_in.at[pl.ds(step * 4, 3)]
        pltpu.make_async_copy(arrived, arrived, relay_sems.at[step]).wait()
        relay_in[step * 4 + x] = part_out[step * 4 + x]
        total = relay_in[step * 4].astype(F32)
        for xs in range(1, 4):
            total = total + relay_in[step * 4 + xs].astype(F32)
        relay_out[step] = total.astype(BF)
        pltpu.make_async_remote_copy(
            src_ref=relay_out.at[step],
            dst_ref=part_in.at[step * 4],
            send_sem=sent_sem.at[0],
            recv_sem=part_sems.at[step],
            device_id={"vol": x * 8 + plane_of(step)},
            device_id_type=MESH,
        ).start()

    lay_at(0)
    lax.fori_loop(0, 2, begin_plane, 0)
    pl.semaphore_wait(barrier, len(met))
    swap = pltpu.make_async_remote_copy(
        src_ref=swap_out,
        dst_ref=swap_in,
        send_sem=swap_sems.at[0],
        recv_sem=swap_sems.at[1],
        device_id=at_zc(0, 1),
        device_id_type=MESH,
    )
    swap.start()
    lax.fori_loop(2, 6, begin_plane, 0)
    swap.wait()
    spec[...] = swap_in[...].astype(F32)
    lay_at(256)
    lax.fori_loop(0, 2, lambda step, carry: finish_plane(step, carry, 1, True), 0)
    lax.fori_loop(2, 6, lambda step, carry: finish_plane(step, carry, 1), 0)
    lax.fori_loop(6, 7, lambda step, carry: finish_plane(step, carry, 0), 0)
    relay(0)
    relay(1)
    lax.fori_loop(7, 8, lambda step, carry: finish_plane(step, carry, 0), 0)
    part_in[28 + x] = part_out[28 + x]

    total = jnp.zeros((32, 128), F32)
    for step in (2, 3, 4, 5, 6, 7, 0, 1):
        tiles = 1 if step < 2 else 4
        arrived = part_in.at[pl.ds(step * 4, tiles if step < 7 else 3)]
        pltpu.make_async_copy(arrived, arrived, part_sems.at[step]).wait()
        for k in range(tiles):
            total = total + part_in[step * 4 + k].astype(F32)
    total = total * scale[...]
    chosen = picks[...]
    upper = total.astype(BF)
    lower = (total - upper.astype(F32)).astype(BF)
    slots = jnp.dot(chosen, upper, preferred_element_type=F32)
    slots = slots + jnp.dot(chosen, lower, preferred_element_type=F32)
    for k in range(32):
        slot_out[k] = slots[4 * k : 4 * k + 4]
    slot_in[y * 4 + x] = slot_out[y * 4 + x]
    for a, b in by_xz:
        pltpu.make_async_remote_copy(
            src_ref=slot_out.at[(y + b) % 8 * 4 + (x + a) % 4],
            dst_ref=slot_in.at[y * 4 + x],
            send_sem=slot_sems.at[0],
            recv_sem=slot_sems.at[1],
            device_id=at_xy(a, b),
            device_id_type=MESH,
        ).start()
    arrived = slot_in.at[pl.ds(0, 31)]
    pltpu.make_async_copy(arrived, arrived, slot_sems.at[1]).wait()
    for xs in range(4):
        chunk = slot_in[xs]
        for ys in range(1, 8):
            chunk = chunk + slot_in[ys * 4 + xs]
        for k in range(2):
            tile[k, 2 * xs : 2 * xs + 2, :] = chunk[2 * k : 2 * k + 2]

    for k in range(2):
        residue = (z - own_begins[k] + NF) % 8
        whole = tile[k]
        for zt in range(8):
            last_out[zt * 2 + k] = jnp.where(residue == zt, 1.0, 0.0) * whole
    last_in[z * 2 + core] = last_out[z * 2 + core]
    for a, b in by_zc:
        pltpu.make_async_remote_copy(
            src_ref=last_out.at[(z + a) % 8 * 2 + (core + b) % 2],
            dst_ref=last_in.at[z * 2 + core],
            send_sem=last_sems.at[0],
            recv_sem=last_sems.at[1],
            device_id=at_zc(a, b),
            device_id_type=MESH,
        ).start()
    arrived = last_in.at[pl.ds(0, 15)]
    pltpu.make_async_copy(arrived, arrived, last_sems.at[1]).wait()
    whole = last_in[0]
    for k in range(1, 16):
        whole = whole + last_in[k]
    out_ref[...] = whole

    sent = part_out.at[pl.ds(0, 31)]
    pltpu.make_async_copy(sent, sent, sent_sem.at[0]).wait()
    sent = slot_out.at[pl.ds(0, 31)]
    pltpu.make_async_copy(sent, sent, slot_sems.at[0]).wait()
    sent = last_out.at[pl.ds(0, 15)]
    pltpu.make_async_copy(sent, sent, last_sems.at[0]).wait()


def per_device(series, send_rows, bin_counts, observer_cells):
    in_vmem = pl.BlockSpec(memory_space=pltpu.VMEM)
    chunks = pl.pallas_call(
        kernel,
        out_shape=jax.ShapeDtypeStruct((8, 128), F32),
        in_specs=[pl.BlockSpec(memory_space=pl.ANY)] * 5,
        out_specs=in_vmem,
        scratch_shapes=[
            pltpu.SMEM((16,), jnp.int32),
            pltpu.VMEM((64, NQ * NT), BF),
            pltpu.VMEM((1, 64), jnp.int32),
            pltpu.VMEM((2, OBS), jnp.int32),
            pltpu.VMEM((2 * NF, NT), BF),
            pltpu.VMEM((1024, 128), F32),
            pltpu.VMEM((1024, 128), BF),
            pltpu.VMEM((1024, 128), BF),
            pltpu.VMEM((3, 128, 128), F32),
            pltpu.VMEM((3, 8, OBS), F32),
            pltpu.VMEM((8, OBS), F32),
            pltpu.VMEM((32, 128, OBS), BF),
            pltpu.VMEM((8, 8, 16, 512), BF),
            pltpu.VMEM((6, 8, 16, OBS), F32),
            pltpu.VMEM((128, 32), BF),
            pltpu.VMEM((32, 128), F32),
            pltpu.VMEM((2, 32, 256), F32),
            pltpu.VMEM((32, 32, 128), BF),
            pltpu.VMEM((32, 32, 128), BF),
            pltpu.VMEM((2, 32, 128), BF),
            pltpu.VMEM((8, 32, 128), BF),
            pltpu.VMEM((32, 4, 128), F32),
            pltpu.VMEM((32, 4, 128), F32),
            pltpu.VMEM((2, 8, 128), F32),
            pltpu.VMEM((16, 8, 128), F32),
            pltpu.VMEM((16, 8, 128), F32),
            pltpu.SemaphoreType.DMA((2,)),
            pltpu.SemaphoreType.DMA((1,)),
            pltpu.SemaphoreType.DMA((8,)),
            pltpu.SemaphoreType.DMA((2,)),
            pltpu.SemaphoreType.DMA((2,)),
            pltpu.SemaphoreType.DMA((2,)),
            pltpu.SemaphoreType.DMA((5,)),
        ],
        compiler_params=pltpu.CompilerParams(
            collective_id=0, has_side_effects=True, vmem_limit_bytes=56 << 20
        ),
    )(
        bin_counts,
        series,
        send_rows.reshape(1, -1),
        observer_cells,
        jnp.asarray(dft_rows()),
    )
    return chunks.reshape(4, 2, 128).transpose(1, 0, 2).reshape(1, 1, 2, OBS)


def solution(mesh):
    placed = (P(("vol", "nar"), None), P("vol", "nar", None), P(), P())
    return jax.shard_map(
        per_device,
        mesh=mesh,
        in_specs=placed,
        out_specs=P("nar", "vol", None, None),
        check_vma=False,
    )
```

```python
import math

import jax
import jax.numpy as jnp
import ml_dtypes
import numpy as np
from jax import lax
from jax.experimental import pallas as pl
from jax.experimental.pallas import tpu as pltpu
from jax.sharding import PartitionSpec as P

NT = 512
NF = 256
NQ = 4
OBS = 512
WAVE_STEP = 0.05
BF = jnp.bfloat16
F32 = jnp.float32
MESH = pl.DeviceIdType.MESH


def dft_rows():
    steps = np.arange(NT, dtype=np.int64)
    turns = (np.arange(1, NF + 1, dtype=np.int64)[:, None] * steps[None, :]) % NT
    angle = turns.astype(np.float32) * np.float32(2.0 * math.pi / NT)
    table = np.stack([np.cos(angle), -np.sin(angle)], axis=1)
    return table.reshape(2 * NF, NT).astype(ml_dtypes.bfloat16)


SIN_TERMS = [(-1.0) ** i / math.factorial(2 * i + 1) for i in range(6)]
COS_TERMS = [(-1.0) ** i / math.factorial(2 * i) for i in range(7)]


def polynomial(terms, square):
    total = terms[-1]
    for term in terms[-2::-1]:
        total = total * square + term
    return total


def cos_sin(turns):
    half = (turns - jnp.round(turns)) * math.pi
    square = half * half
    s = half * polynomial(SIN_TERMS, square)
    c = polynomial(COS_TERMS, square)
    return 1.0 - 2.0 * s * s, 2.0 * s * c


def times(one, other):
    return one[0] * other[0] - one[1] * other[1], one[0] * other[1] + one[1] * other[0]


def squared(one):
    return 1.0 - 2.0 * one[1] * one[1], 2.0 * one[0] * one[1]


def modulo(value, base):
    rest = value - (value.astype(F32) * (1.0 / base)).astype(jnp.int32) * base
    rest = jnp.where(rest < 0, rest + base, rest)
    return jnp.where(rest >= base, rest - base, rest)


def kernel(
    counts_hbm,
    series_hbm,
    listing_hbm,
    cells_hbm,
    dft_hbm,
    out_ref,
    counts_ref,
    series_ref,
    listing_ref,
    cells_ref,
    dft_ref,
    spec,
    swap_out,
    swap_in,
    place,
    facing,
    weight,
    table,
    coef,
    begun,
    picks,
    scale,
    stage,
    part_out,
    part_in,
    relay_out,
    relay_in,
    slot_out,
    slot_in,
    tile,
    last_out,
    last_in,
    swap_sems,
    sent_sem,
    part_sems,
    relay_sems,
    slot_sems,
    last_sems,
    load_sems,
):
    u = lax.axis_index("vol")
    n = lax.axis_index("nar")
    x, z = u // 8, u % 8
    core = n % 2
    y = n // 2
    nars = 16

    loads = [
        pltpu.make_async_copy(source, target, load_sems.at[i])
        for i, (source, target) in enumerate(
            (
                (cells_hbm, cells_ref),
                (counts_hbm, counts_ref),
                (listing_hbm, listing_ref),
                (series_hbm, series_ref),
                (dft_hbm, dft_ref),
            )
        )
    ]
    for load in loads:
        load.start()

    barrier = pltpu.get_barrier_semaphore()

    by_xz = [(a, b) for a in range(4) for b in range(8) if a or b]
    by_xz.sort(key=lambda k: -min(k[0], 4 - k[0]) - min(k[1], 8 - k[1]))
    by_zc = [(a, b) for a in range(8) for b in range(2) if a or b]
    by_zc.sort(key=lambda k: -min(k[0], 8 - k[0]) - k[1])

    def at_xz(a, b):
        return {"vol": (x + a) % 4 * 8 + (z + b) % 8}

    def at_xy(a, b):
        return {"vol": (x + a) % 4 * 8 + z, "nar": (y + b) % 8 * 2 + core}

    def at_zc(a, b):
        return {"vol": x * 8 + (z + a) % 8, "nar": y * 2 + (core + b) % 2}

    met = [(*k, 0, 0) for k in by_xz]
    met += [(k[0], 0, k[1], 0) for k in by_xz if k[1]]
    met += [(0, k[0], 0, k[1]) for k in by_zc if k[1]]
    met.sort(key=lambda k: -min(k[0], 4 - k[0]) - min(k[1], 8 - k[1]) - min(k[2], 8 - k[2]))
    for a, b, c, d in met:
        other = {
            "vol": (x + a) % 4 * 8 + (z + b) % 8,
            "nar": (y + c) % 8 * 2 + (core + d) % 2,
        }
        pl.semaphore_signal(barrier, inc=1, device_id=other, device_id_type=MESH)

    loads[0].wait()
    slab = u * 8 + n // 2
    point = slab * 128 + (lax.broadcasted_iota(jnp.int32, (128, 128), 0) + 64 * core) % 128
    c, s = cos_sin(modulo(point * 1597, 8191).astype(F32) * (1.0 / 8191.0))
    place[0] = 20.0 * c
    place[1] = 20.0 * s
    place[2] = slab.astype(F32) * 0.5 + modulo(point * 613, 127).astype(F32) * (0.37 / 127.0)
    cells = cells_ref[...].astype(F32)
    polar = cos_sin((cells[0:1] + 0.5) * (1.0 / 256.0))
    azimuth = cos_sin(cells[1:2] * (1.0 / 128.0))
    facing[0] = jnp.broadcast_to(polar[1] * azimuth[0], (8, OBS))
    facing[1] = jnp.broadcast_to(polar[1] * azimuth[1], (8, OBS))
    facing[2] = jnp.broadcast_to(polar[0], (8, OBS))
    term = lax.broadcasted_iota(jnp.int32, (8, OBS), 0) % NQ
    weight[...] = jnp.where(
        term == 0,
        1.0,
        jnp.where(term == 1, facing[0], jnp.where(term == 2, facing[1], facing[2])),
    )

    def fill(at, carry):
        rows16 = pl.ds(pl.multiple_of((at // 2) * 16, 16), 16)
        lanes = pl.ds(pl.multiple_of((at % 2) * 256, 256), 256)
        dotted = 0.0
        for axis in range(3):
            spot = place[axis, rows16, :]
            look = facing[axis, :, lanes]
            dotted = dotted + jnp.concatenate([spot, spot], axis=1) * jnp.concatenate([look, look], axis=0)
        turns = dotted * (WAVE_STEP / (2.0 * math.pi))

        def keep(index, value):
            table[index, rows16, lanes] = value[0].astype(BF)
            table[index + 1, rows16, lanes] = value[1].astype(BF)

        def onward(index, before, now, step):
            twice = 2.0 * step[0]
            keep(index, now)
            for k in range(1, 8):
                after = twice * now[0] - before[0], twice * now[1] - before[1]
                before, now = now, after
                keep(index + 2 * k, now)

        step = cos_sin(turns)
        coarse = cos_sin(turns * (core.astype(F32) * 128.0 + 61.0))
        onward(0, times(coarse, (step[0], -step[1])), coarse, step)
        fine = squared(squared(step))
        onward(16, (fine[0], -fine[1]), fine, squared(fine))
        return carry

    lax.fori_loop(0, 16, fill, 0)

    loads[1].wait()
    row = lax.broadcasted_iota(jnp.int32, (128, 32), 0)
    col = lax.broadcasted_iota(jnp.int32, (128, 32), 1)
    bin_of = core * 128 + col // 2 * 8 + z
    owner = row // 16 * 2 + row % 4 // 2
    begin, begins, counts = jnp.int32(0), jnp.zeros_like(row), jnp.zeros_like(row)
    own_begins = [jnp.int32(0), jnp.int32(0)]
    for m in range(nars):
        amount = counts_ref[m]
        begins = jnp.where(owner == m, begin, begins)
        counts = jnp.where(owner == m, amount, counts)
        for k in range(2):
            own_begins[k] = own_begins[k] + jnp.where(m < 2 * y + k, amount, 0)
        begin = begin + amount
    seat = bin_of - begins
    ahead = seat - row // 4 % 4 * 8
    chosen = (row % 2 == col % 2) & (ahead >= 0) & (ahead < 8) & (seat < counts)
    picks[...] = jnp.where(chosen, 1.0, 0.0).astype(BF)
    r = lax.broadcasted_iota(jnp.int32, (32, 128), 0)
    b = core * 128 + r // 2 * 8 + z
    amount = (b + 1).astype(F32) * (1.0 / math.sqrt(32768.0) / NF)
    scale[...] = jnp.where(r % 2 == 0, -amount, amount)

    for load in loads[2:]:
        load.wait()
    pick = lax.broadcasted_iota(jnp.int32, (64, 64), 0) == listing_ref[...]
    surface = lax.dot_general(
        jnp.where(pick, 1.0, 0.0).astype(BF),
        series_ref[...],
        (((0,), (0,)), ((), ())),
        preferred_element_type=F32,
    ).astype(BF)
    rows = jnp.concatenate([surface[:, q * NT : (q + 1) * NT] for q in range(NQ)], axis=0)

    def transform(half):
        lines = dft_ref[pl.ds(pl.multiple_of(half * 256, 256), 256), :]
        spectra = lax.dot_general(lines, rows, (((1,), (1,)), ((), ())), preferred_element_type=F32)
        spectra = spectra * (1.0 / math.sqrt(NT))
        first = lax.broadcasted_iota(jnp.int32, (256, 128), 1) < 64
        for q in range(NQ):
            both = spectra[:, q // 2 * 128 : q // 2 * 128 + 128]
            flipped = pltpu.roll(both, 64, 1)
            twice = jnp.where(first, flipped, both) if q % 2 else jnp.where(first, both, flipped)
            spec[pl.ds(q, 256, stride=NQ), :] = twice

    transform(1 - core)
    swap_out[...] = spec[...].astype(BF)
    transform(core)

    sign = jnp.where(lax.broadcasted_iota(jnp.int32, (8, 128), 0) < 4, 1.0, -1.0)
    turn = jnp.where(lax.broadcasted_iota(jnp.int32, (8, 128), 1) < 64, 1.0, -1.0)

    def lay_at(lane):
        def lay(r, carry):
            for j in range(8):
                high = spec[pl.ds(pl.multiple_of((r + 8 * (8 + j)) * 8, 8), 8), :]
                low = spec[pl.ds(pl.multiple_of((r + 8 * (7 - j)) * 8, 8), 8), :]
                high2 = pltpu.roll(high, 4, 0) * sign
                low2 = pltpu.roll(low, 4, 0) * sign
                blocks = ((high * turn, low), (high2, low2 * turn))
                for k, both in enumerate(blocks):
                    lanes = pl.ds(lane + k * 128, 128)
                    coef[r, j, :, lanes] = jnp.concatenate(both, axis=0).astype(BF)
            return carry

        lax.fori_loop(0, 8, lay, 0)

    def plane_of(step):
        return (z + 4 + (1 - 2 * (step % 2)) * ((step + 1) // 2)) % 8

    def products(zt, j, lanes, first, last):
        green = []
        for block in range(first, last):
            points = pl.ds(block * 64, 64)
            c, s = table[2 * zt, points, lanes], table[2 * zt + 1, points, lanes]
            fc, fs = table[16 + 2 * j, points, lanes], table[17 + 2 * j, points, lanes]
            green += [c * fc, s * fs, s * fc, c * fs]
        left = coef[zt, j, :, pl.ds(first * 256, (last - first) * 256)]
        return jnp.dot(left, jnp.concatenate(green, axis=0), preferred_element_type=F32)

    def begin_plane(step, carry):
        zt = plane_of(step)
        for half in range(2):
            lanes = pl.ds(half * 256, 256)
            for j in range(8):
                begun[step - 3, j, :, lanes] = products(zt, j, lanes, 0, 1)
        return carry

    def finish_plane(step, carry, first, relayed=False):
        zt = plane_of(step)
        for part in range(2):
            half = (x // 2 + 1 + part) % 2
            lanes = pl.ds(pl.multiple_of(half * 256, 256), 256)
            for j in range(8):
                sums = products(zt, j, lanes, first, 2)
                if first:
                    sums = sums + begun[step - 3, j, :, lanes]
                for sg, k in enumerate((8 + j, 7 - j)):
                    total = sums[8 * sg : 8 * sg + 8] * weight[:, lanes]
                    total = total + pltpu.roll(total, 7, 0)
                    total = total + pltpu.roll(total, 6, 0)
                    stage[part, 2 * k : 2 * k + 1, :] = total[4:5]
                    stage[part, 2 * k + 1 : 2 * k + 2, :] = total[0:1]
            for k in range(2):
                xt = 2 * half + (x + 1 + k) % 2
                chosen = jnp.where((x + 1 + k) % 2 == 0, stage[part, :, 0:128], stage[part, :, 128:256])
                part_out[step * 4 + xt] = chosen.astype(BF)

                def send(xt=xt):
                    pltpu.make_async_remote_copy(
                        src_ref=part_out.at[step * 4 + xt],
                        dst_ref=(relay_in if relayed else part_in).at[step * 4 + x],
                        send_sem=sent_sem.at[0],
                        recv_sem=(relay_sems if relayed else part_sems).at[step],
                        device_id={"vol": xt * 8 + (z if relayed else zt)},
                        device_id_type=MESH,
                    ).start()

                if part == 1 and k == 1:
                    if not relayed:
                        pl.when(step < 7)(send)
                else:
                    send()
        return carry

    def relay(step):
        arrived = relay_in.at[pl.ds(step * 4, 3)]
        pltpu.make_async_copy(arrived, arrived, relay_sems.at[step]).wait()
        relay_in[step * 4 + x] = part_out[step * 4 + x]
        total = relay_in[step * 4].astype(F32)
        for xs in range(1, 4):
            total = total + relay_in[step * 4 + xs].astype(F32)
        relay_out[step] = total.astype(BF)
        pltpu.make_async_remote_copy(
            src_ref=relay_out.at[step],
            dst_ref=part_in.at[step * 4],
            send_sem=sent_sem.at[0],
            recv_sem=part_sems.at[step],
            device_id={"vol": x * 8 + plane_of(step)},
            device_id_type=MESH,
        ).start()

    lay_at(0)
    lax.fori_loop(3, 5, begin_plane, 0)
    pl.semaphore_wait(barrier, len(met))
    swap = pltpu.make_async_remote_copy(
        src_ref=swap_out,
        dst_ref=swap_in,
        send_sem=swap_sems.at[0],
        recv_sem=swap_sems.at[1],
        device_id=at_zc(0, 1),
        device_id_type=MESH,
    )
    swap.start()
    lax.fori_loop(5, 8, begin_plane, 0)
    swap.wait()
    spec[...] = swap_in[...].astype(F32)
    lay_at(256)
    lax.fori_loop(0, 2, lambda step, carry: finish_plane(step, carry, 0, True), 0)
    lax.fori_loop(2, 3, lambda step, carry: finish_plane(step, carry, 0), 0)
    lax.fori_loop(3, 6, lambda step, carry: finish_plane(step, carry, 1), 0)
    lax.fori_loop(6, 7, lambda step, carry: finish_plane(step, carry, 1), 0)
    relay(0)
    relay(1)
    lax.fori_loop(7, 8, lambda step, carry: finish_plane(step, carry, 1), 0)
    part_in[28 + x] = part_out[28 + x]

    total = jnp.zeros((32, 128), F32)
    for step in (2, 3, 4, 5, 6, 7, 0, 1):
        tiles = 1 if step < 2 else 4
        arrived = part_in.at[pl.ds(step * 4, tiles if step < 7 else 3)]
        pltpu.make_async_copy(arrived, arrived, part_sems.at[step]).wait()
        for k in range(tiles):
            total = total + part_in[step * 4 + k].astype(F32)
    total = total * scale[...]
    chosen = picks[...]
    upper = total.astype(BF)
    lower = (total - upper.astype(F32)).astype(BF)
    slots = jnp.dot(chosen, upper, preferred_element_type=F32)
    slots = slots + jnp.dot(chosen, lower, preferred_element_type=F32)
    for k in range(32):
        slot_out[k] = slots[4 * k : 4 * k + 4]
    slot_in[y * 4 + x] = slot_out[y * 4 + x]
    for a, b in by_xz:
        pltpu.make_async_remote_copy(
            src_ref=slot_out.at[(y + b) % 8 * 4 + (x + a) % 4],
            dst_ref=slot_in.at[y * 4 + x],
            send_sem=slot_sems.at[0],
            recv_sem=slot_sems.at[1],
            device_id=at_xy(a, b),
            device_id_type=MESH,
        ).start()
    arrived = slot_in.at[pl.ds(0, 31)]
    pltpu.make_async_copy(arrived, arrived, slot_sems.at[1]).wait()
    for xs in range(4):
        chunk = slot_in[xs]
        for ys in range(1, 8):
            chunk = chunk + slot_in[ys * 4 + xs]
        for k in range(2):
            tile[k, 2 * xs : 2 * xs + 2, :] = chunk[2 * k : 2 * k + 2]

    for k in range(2):
        residue = (z - own_begins[k] + NF) % 8
        whole = tile[k]
        for zt in range(8):
            last_out[zt * 2 + k] = jnp.where(residue == zt, 1.0, 0.0) * whole
    last_in[z * 2 + core] = last_out[z * 2 + core]
    for a, b in by_zc:
        pltpu.make_async_remote_copy(
            src_ref=last_out.at[(z + a) % 8 * 2 + (core + b) % 2],
            dst_ref=last_in.at[z * 2 + core],
            send_sem=last_sems.at[0],
            recv_sem=last_sems.at[1],
            device_id=at_zc(a, b),
            device_id_type=MESH,
        ).start()
    arrived = last_in.at[pl.ds(0, 15)]
    pltpu.make_async_copy(arrived, arrived, last_sems.at[1]).wait()
    whole = last_in[0]
    for k in range(1, 16):
        whole = whole + last_in[k]
    out_ref[...] = whole

    sent = part_out.at[pl.ds(0, 31)]
    pltpu.make_async_copy(sent, sent, sent_sem.at[0]).wait()
    sent = slot_out.at[pl.ds(0, 31)]
    pltpu.make_async_copy(sent, sent, slot_sems.at[0]).wait()
    sent = last_out.at[pl.ds(0, 15)]
    pltpu.make_async_copy(sent, sent, last_sems.at[0]).wait()


def per_device(series, send_rows, bin_counts, observer_cells):
    in_vmem = pl.BlockSpec(memory_space=pltpu.VMEM)
    chunks = pl.pallas_call(
        kernel,
        out_shape=jax.ShapeDtypeStruct((8, 128), F32),
        in_specs=[pl.BlockSpec(memory_space=pl.ANY)] * 5,
        out_specs=in_vmem,
        scratch_shapes=[
            pltpu.SMEM((16,), jnp.int32),
            pltpu.VMEM((64, NQ * NT), BF),
            pltpu.VMEM((1, 64), jnp.int32),
            pltpu.VMEM((2, OBS), jnp.int32),
            pltpu.VMEM((2 * NF, NT), BF),
            pltpu.VMEM((1024, 128), F32),
            pltpu.VMEM((1024, 128), BF),
            pltpu.VMEM((1024, 128), BF),
            pltpu.VMEM((3, 128, 128), F32),
            pltpu.VMEM((3, 8, OBS), F32),
            pltpu.VMEM((8, OBS), F32),
            pltpu.VMEM((32, 128, OBS), BF),
            pltpu.VMEM((8, 8, 16, 512), BF),
            pltpu.VMEM((5, 8, 16, OBS), F32),
            pltpu.VMEM((128, 32), BF),
            pltpu.VMEM((32, 128), F32),
            pltpu.VMEM((2, 32, 256), F32),
            pltpu.VMEM((32, 32, 128), BF),
            pltpu.VMEM((32, 32, 128), BF),
            pltpu.VMEM((2, 32, 128), BF),
            pltpu.VMEM((8, 32, 128), BF),
            pltpu.VMEM((32, 4, 128), F32),
            pltpu.VMEM((32, 4, 128), F32),
            pltpu.VMEM((2, 8, 128), F32),
            pltpu.VMEM((16, 8, 128), F32),
            pltpu.VMEM((16, 8, 128), F32),
            pltpu.SemaphoreType.DMA((2,)),
            pltpu.SemaphoreType.DMA((1,)),
            pltpu.SemaphoreType.DMA((8,)),
            pltpu.SemaphoreType.DMA((2,)),
            pltpu.SemaphoreType.DMA((2,)),
            pltpu.SemaphoreType.DMA((2,)),
            pltpu.SemaphoreType.DMA((5,)),
        ],
        compiler_params=pltpu.CompilerParams(
            collective_id=0, has_side_effects=True, vmem_limit_bytes=56 << 20
        ),
    )(
        bin_counts,
        series,
        send_rows.reshape(1, -1),
        observer_cells,
        jnp.asarray(dft_rows()),
    )
    return chunks.reshape(4, 2, 128).transpose(1, 0, 2).reshape(1, 1, 2, OBS)


def solution(mesh):
    placed = (P(("vol", "nar"), None), P("vol", "nar", None), P(), P())
    return jax.shard_map(
        per_device,
        mesh=mesh,
        in_specs=placed,
        out_specs=P("nar", "vol", None, None),
        check_vma=False,
    )
```
